256 devices in a mesh: tile: 32 (over x, z), band: 8 (over y, core).
Axes of the slice: x: 4, y: 4, z: 8, core: 2. Of those that a mesh axis runs over, the one named last changes fastest.
Arguments:
- members: bfloat16 [64, 128, 65536], P(None, 'band', 'tile'), may hold values from -6 to 6
- modes: float32 [8, 128], replicated, may hold values from -4 to 4
- obs_cell: int32 [2097152], P(('tile', 'band')), may hold values from 0 to 2047
- obs_level: int32 [2097152], P(('tile', 'band')), may hold values from 0 to 15
- obs_side: int32 [2097152], P(('tile', 'band')), may hold values from 0 to 1
- obs_weight: float32 [2097152], P(('tile', 'band')), may hold values from 0.1 to 0.9
- obs_scale: float32 [2097152], P(('tile', 'band')), may hold values from 0.01 to 0.05
- innovation: float32 [2097152], P(('tile', 'band')), may hold values from -6 to 6
Outputs:
- increment: float32 [128, 65536], P('band', 'tile')
- analysis: bfloat16 [64, 128, 65536], P(None, 'band', 'tile')
The draws below stay inside these ranges and needn't reach their ends.
All inputs are finite; a program needn't handle non-finite values.
Results may differ from the reference program's by a relative error of at most 0.0087.
Values may be sent and summed in bfloat16 or wider, within the bound.
A program may use at most 128 MiB of HBM per device.

```python
import math
import jax
import jax.numpy as jnp
from jax import lax

MEMBERS = 64
MODES = 8
LEV_DEV = 16
CELLS_DEV = 2048
OBS_DEV = 8192
LEVELS = 128
CELLS = 65536
OBS = 2097152
N_BAND = 8


def signed_loads(key, low, high):
    key_size, key_sign = jax.random.split(key)
    size = jax.random.uniform(key_size, (3, MEMBERS), jnp.float32, low, high)
    flips = jax.random.bernoulli(key_sign, 0.5, (3, MEMBERS)).astype(jnp.float32)
    signs = jnp.concatenate([jnp.ones((1, MEMBERS), jnp.float32), 2.0 * flips[1:] - 1.0], axis=0)
    return size * signs


def draw_members(key, part):
    key = jax.random.fold_in(key, 11)
    key_own, key_common, key_loads = jax.random.split(key, 3)
    common = jax.random.normal(key_common, (3, LEVELS, CELLS), jnp.float32)
    own = jax.random.normal(key_own, (MEMBERS, LEVELS, CELLS), jnp.float32)
    loads = signed_loads(key_loads, 0.3, 1.0)
    total = own + loads[0][:, None, None] * common[0][None]
    total = total + loads[1][:, None, None] * common[1][None]
    total = total + loads[2][:, None, None] * common[2][None]
    return jnp.clip(total, -6.0, 6.0).astype(jnp.bfloat16)


def draw_modes(key, part):
    key = jax.random.fold_in(key, 23)
    key_own, key_profile = jax.random.split(key)
    profile = jax.random.normal(key_profile, (1, LEVELS), jnp.float32)
    own = jax.random.normal(key_own, (MODES, LEVELS), jnp.float32)
    total = own + 0.7 * profile
    return jnp.clip(total, -4.0, 4.0)


def touch_ends(array, key, least, top_value):
    longest = array.shape.index(max(array.shape))
    spots = []
    for shift in (0, 1):
        where = [jax.random.randint(jax.random.fold_in(key, axis), (), 0, length) for axis, length in enumerate(array.shape)]
        where[longest] = (where[longest] + shift) % array.shape[longest]
        spots.append(tuple(where))
    return array.at[spots[0]].set(least).at[spots[1]].set(top_value)


def shard_levels(own_key, dims, shards, least, high):
    loudness, own = 1.0, jax.random.fold_in(own_key, 6)
    for dim, parts in shards:
        heights = jnp.exp(jax.random.uniform(jax.random.fold_in(own, dim), (parts,), jnp.float32, least / len(shards), high / len(shards)))
        loudness = loudness * jnp.repeat(heights, dims[dim] // parts).reshape([-1 if axis == dim else 1 for axis in range(len(dims))])
    return loudness


def bell_draw(rng, extent, spread, limit, shards=(), kind=jnp.bfloat16):
    array = jax.random.normal(rng, extent, jnp.float32) * spread
    if len(shards) > 0:
        array = shard_levels(rng, extent, shards, -0.22, 0.18) * array
    return jnp.clip(array, min=-limit, max=limit).astype(kind)


def setup_inputs(seed: int = 0) -> dict:
    arg_keys = jax.random.split(jax.random.key(seed), 9)
    members = draw_members(jax.random.fold_in(arg_keys[8], 71), 0)
    modes = draw_modes(jax.random.fold_in(arg_keys[8], 71), 0)
    obs_cell = touch_ends(jax.random.randint(arg_keys[2], (OBS,), 0, CELLS_DEV), jax.random.fold_in(arg_keys[2], 1), 0, CELLS_DEV - 1).astype(jnp.int32)
    obs_level = touch_ends(jax.random.randint(arg_keys[3], (OBS,), 0, LEV_DEV), jax.random.fold_in(arg_keys[3], 1), 0, LEV_DEV - 1).astype(jnp.int32)
    obs_side = touch_ends(jax.random.randint(arg_keys[4], (OBS,), 0, 2), jax.random.fold_in(arg_keys[4], 1), 0, 1).astype(jnp.int32)
    obs_weight = jnp.clip(0.1 + 0.79999997 * jax.random.uniform(arg_keys[5], (OBS,), jnp.float32) ** shard_levels(arg_keys[5], (OBS,), ((0, 256),), -0.2, 0.2), 0.1, 0.9)
    obs_scale = jnp.clip(jnp.exp(math.log(0.05) - 1.609438 * jax.random.uniform(arg_keys[6], (OBS,), jnp.float32) ** shard_levels(arg_keys[6], (OBS,), ((0, 256),), -0.2, 0.2)), 0.01, 0.05)
    innovation = bell_draw(arg_keys[7], (OBS,), 1.0, 6.0, ((0, 256),), jnp.float32)
    return dict(members=members, modes=modes, obs_cell=obs_cell, obs_level=obs_level, obs_side=obs_side, obs_weight=obs_weight, obs_scale=obs_scale, innovation=innovation)


def reference(members, modes, obs_cell, obs_level, obs_side, obs_weight, obs_scale, innovation):
    n_members = members.shape[0]
    n_modes = modes.shape[0]
    levels = members.shape[1]
    cells = members.shape[2]
    ens = n_members * n_modes
    flat = members.reshape(n_members, levels * cells)
    grid = lax.iota(jnp.int32, levels)
    blocks = obs_cell.shape[0] // OBS_DEV

    def block_sums(carry, index):
        gram, cross, drive = carry
        start = (index * OBS_DEV).astype(jnp.int32)
        cell = lax.dynamic_slice_in_dim(obs_cell, start, OBS_DEV)
        level = lax.dynamic_slice_in_dim(obs_level, start, OBS_DEV)
        side = lax.dynamic_slice_in_dim(obs_side, start, OBS_DEV)
        weight = lax.dynamic_slice_in_dim(obs_weight, start, OBS_DEV)
        scale = lax.dynamic_slice_in_dim(obs_scale, start, OBS_DEV)
        innov = lax.dynamic_slice_in_dim(innovation, start, OBS_DEV)
        tile = index // N_BAND
        band = index % N_BAND
        gcell = tile * CELLS_DEV + cell
        near_level = band * LEV_DEV + level
        far_level = near_level + 2 * side - 1
        valid = ((far_level >= 0) & (far_level < levels)).astype(jnp.float32)
        far_clip = jnp.clip(far_level, 0, levels - 1).astype(jnp.int32)
        near = jnp.take(flat, (near_level * cells + gcell).astype(jnp.int32), axis=1).astype(jnp.float32)
        far = jnp.take(flat, (far_clip * cells + gcell).astype(jnp.int32), axis=1).astype(jnp.float32) * valid[None, :]
        near_pick = (grid[:, None] == near_level[None, :]).astype(jnp.float32)
        far_pick = (grid[:, None] == far_level[None, :]).astype(jnp.float32)
        near_mode = jnp.dot(modes, near_pick, precision=lax.Precision.HIGHEST)
        far_mode = jnp.dot(modes, far_pick, precision=lax.Precision.HIGHEST)
        keep = 1.0 - weight
        perturb = scale * (keep * near[:, None, :] * near_mode[None] + weight * far[:, None, :] * far_mode[None])
        perturb = perturb.reshape(ens, OBS_DEV).astype(jnp.bfloat16)
        plain = (scale * (keep * near + weight * far)).astype(jnp.bfloat16)
        scaled = (scale * innov).astype(jnp.bfloat16)
        gram = gram + lax.dot_general(perturb.astype(jnp.float32), perturb.astype(jnp.float32), (((1,), (1,)), ((), ())), preferred_element_type=jnp.float32)
        cross = cross + lax.dot_general(perturb.astype(jnp.float32), plain.astype(jnp.float32), (((1,), (1,)), ((), ())), preferred_element_type=jnp.float32)
        drive = drive + jnp.dot(perturb.astype(jnp.float32), scaled.astype(jnp.float32), preferred_element_type=jnp.float32)
        return ((gram, cross, drive), None)
    start_sums = (jnp.zeros((ens, ens), jnp.float32), jnp.zeros((ens, n_members), jnp.float32), jnp.zeros((ens,), jnp.float32))
    (gram, cross, drive), _ = lax.scan(block_sums, start_sums, jnp.arange(blocks, dtype=jnp.int32))
    gram = gram + float(ens - 1) * jnp.eye(ens, dtype=jnp.float32)
    lower = jnp.linalg.cholesky(gram)
    rhs = jnp.concatenate([drive[:, None], cross], axis=1)
    first = lax.linalg.triangular_solve(lower, rhs, left_side=True, lower=True)
    solved = lax.linalg.triangular_solve(lower, first, left_side=True, lower=True, transpose_a=True)
    mean_weights = jnp.einsum('pj,jl->lp', solved[:, 0].reshape(n_members, n_modes), modes, precision=lax.Precision.HIGHEST).astype(jnp.bfloat16)
    member_weights = jnp.einsum('pjk,jl->lpk', solved[:, 1:].reshape(n_members, n_modes, n_members), modes, precision=lax.Precision.HIGHEST).astype(jnp.bfloat16)

    def one_level(level):
        rows = lax.dynamic_index_in_dim(members, level, 1, keepdims=False).astype(jnp.float32)
        mean_row = lax.dynamic_index_in_dim(mean_weights, level, 0, keepdims=False).astype(jnp.float32)
        weight_block = lax.dynamic_index_in_dim(member_weights, level, 0, keepdims=False).astype(jnp.float32)
        inc = jnp.dot(mean_row, rows, precision=lax.Precision.HIGHEST)
        correction = jnp.dot(weight_block.T, rows, precision=lax.Precision.HIGHEST)
        return (inc, (rows - correction).astype(jnp.bfloat16))
    increment, analysis = lax.map(one_level, jnp.arange(levels, dtype=jnp.int32))
    return (increment, jnp.transpose(analysis, (1, 0, 2)))
```

```python
import jax
import jax.numpy as jnp
from jax import lax
from jax.experimental import pallas as pl
from jax.experimental.pallas import tpu as pltpu
from jax.sharding import PartitionSpec as P

BF = jnp.bfloat16
F32 = jnp.float32
VM = pl.BlockSpec(memory_space=pltpu.VMEM)
NT = (((1,), (1,)), ((), ()))
ROWS = 1792
HALF = ROWS // 2
PIECE = HALF // 16


def scatter_kernel(cell_ref, level_ref, side_ref, weight_ref, scale_ref, innov_ref, field_ref, lhs_s, hot_s):
    field_ref[...] = jnp.zeros_like(field_ref)
    rows16 = lax.broadcasted_iota(jnp.int32, (16, 128), 0).astype(F32)
    zero = jnp.zeros((16, 128), BF)
    one = jnp.ones((16, 128), BF)

    def chunk(i, _):
        sl = pl.ds(pl.multiple_of(i * 8, 8), 8)
        cell = cell_ref[sl, :]
        lev = level_ref[sl, :]
        side = side_ref[sl, :]
        w = weight_ref[sl, :]
        s = scale_ref[sl, :]
        ch = cell >> 8
        cl8 = (cell & 255).astype(F32)
        kn8 = ((lev + 1) * 8 + ch).astype(F32)
        kf8 = ((lev + 2 * side) * 8 + ch).astype(F32)
        kp8 = ((lev + side) * 8 + ch).astype(F32)
        a = s * (1.0 - w)
        b = s * w
        t = s * innov_ref[sl, :]

        def split(v):
            hi = v.astype(BF).astype(F32)
            return hi, v - hi

        vals = [split(v) for v in (a * a, b * b, a * b, a * t, b * t)]
        for k in range(8):
            cols = slice(128 * k, 128 * k + 128)

            def wide(v):
                return jnp.broadcast_to(v[k : k + 1, :], (16, 128)).astype(BF)

            cl, kn, kf, kp = wide(cl8), wide(kn8), wide(kf8), wide(kp8)
            dn, df, e, gn, gf = [(wide(h), wide(l)) for h, l in vals]
            for g in range(9):
                it = (rows16 + 16.0 * g).astype(BF)
                mn = it == kn
                mf = it == kf
                mp = it == kp
                for h in range(2):
                    at = 144 * h + 16 * g
                    lhs_s[pl.ds(at, 16), cols] = jnp.where(mn, dn[h], jnp.where(mf, df[h], zero))
                    lhs_s[pl.ds(288 + at, 16), cols] = jnp.where(mn, gn[h], jnp.where(mf, gf[h], zero))
                    lhs_s[pl.ds(576 + at, 16), cols] = jnp.where(mp, e[h], zero)
            for g in range(16):
                it = (rows16 + 16.0 * g).astype(BF)
                hot_s[pl.ds(16 * g, 16), cols] = jnp.where(it == cl, one, zero)
        field_ref[...] += lax.dot_general(lhs_s[...], hot_s[...], NT, preferred_element_type=F32)
        return 0

    lax.fori_loop(0, 8, chunk, 0)


def sums_kernel(field_ref, mem_ref, lo_ref, hi_ref, modes_ref, out_ref, x32_s, stack_s, prod_s, coef_s):
    def conv(m, _):
        v = mem_ref[m].astype(F32)
        for k in range(16):
            x32_s[k, pl.ds(pl.multiple_of(m * 16, 16), 16), :] = v[:, 128 * k:128 * k + 128]
        return 0
    lax.fori_loop(0, 64, conv, 0, unroll=2)

    first = lax.broadcasted_iota(jnp.int32, (16, 128), 0)

    def level(r, k):
        if r == 0:
            return lo_ref[:, 128 * k:128 * k + 128].astype(F32)
        if r == 17:
            return hi_ref[:, 128 * k:128 * k + 128].astype(F32)
        return x32_s[k, pl.ds(r - 1, 64, stride=16), :]

    def field(f, r, k):
        row, ls = 288 * f + 8 * r + k // 2, slice(128 * (k % 2), 128 * (k % 2) + 128)
        return field_ref[pl.ds(row, 1), ls] + field_ref[pl.ds(row + 144, 1), ls]

    for q in range(9):
        for k in range(16):
            cs = slice(128 * k, 128 * k + 128)
            xs = {r: level(r, k) for r in range(max(2 * q - 1, 0), min(2 * q + 3, 18))}
            es = {r: field(2, r, k) for r in range(max(2 * q - 1, 0), min(2 * q + 2, 17))}
            for h in range(2):
                r = 2 * q + h
                base = 208 * h
                x = xs[r]
                stack_s[pl.ds(416 + 64 * h, 64), cs] = x.astype(BF)
                stack_s[pl.ds(base, 64), cs] = (x * field(0, r, k)).astype(BF)
                zero = jnp.zeros((64, 128), BF)
                stack_s[pl.ds(base + 64, 64), cs] = (xs[r - 1] * es[r - 1]).astype(BF) if r > 0 else zero
                stack_s[pl.ds(base + 128, 64), cs] = (xs[r + 1] * es[r]).astype(BF) if r < 17 else zero
                g = jnp.broadcast_to(field(1, r, k), (16, 128))
                gh = g.astype(BF).astype(F32)
                stack_s[pl.ds(base + 192, 16), cs] = jnp.where(first == 0, gh, jnp.where(first == 1, g - gh, 0.0)).astype(BF)
        p = lax.dot_general(stack_s[pl.ds(0, 416), :], stack_s[pl.ds(416, 128), :], (((1,), (1,)), ((), ())),
                            preferred_element_type=F32)
        lane = lax.broadcasted_iota(jnp.int32, (208, 128), 1)
        prod_s[q] = jnp.where(lane < 64, p[:208], p[208:])

    start = lax.axis_index("band") * 16 - 1
    half = lax.broadcasted_iota(jnp.int32, (1, 128), 1) < 64
    for j in range(9):
        if j < 8:
            phi = []
            for r in range(-1, 19):
                l = start + r
                ok = (l >= 0) & (l < 128)
                phi.append(jnp.where(ok, modes_ref[j, jnp.clip(l, 0, 127)], 0.0))
        else:
            phi = [jnp.float32(1.0)] * 20
        for q in range(9):
            for s in range(3):
                r = 2 * q + (1, 0, 2)[s]
                coef_s[s, j, pl.ds(q, 1), :] = jnp.where(half, phi[r], phi[r + 1])
    lane8 = lax.broadcasted_iota(jnp.int32, (8, 128), 1) < 64
    def group(i, _):
        s0 = [prod_s[q, pl.ds(i * 8, 8), :] for q in range(9)]
        s1 = [prod_s[q, pl.ds(64 + i * 8, 8), :] for q in range(9)]
        s2 = [prod_s[q, pl.ds(128 + i * 8, 8), :] for q in range(9)]
        row = 0
        for j in range(8):
            t = [s0[q] * coef_s[0, j, pl.ds(q, 1), :] + s1[q] * coef_s[1, j, pl.ds(q, 1), :] + s2[q] * coef_s[2, j, pl.ds(q, 1), :] for q in range(9)]
            def block(jj):
                acc = t[0] * coef_s[0, jj, pl.ds(0, 1), :]
                for q in range(1, 9):
                    acc = acc + t[q] * coef_s[0, jj, pl.ds(q, 1), :]
                return acc
            for pair in range(j // 2, 5):
                u = block(2 * pair)
                u = u + pltpu.roll(u, 64, 1)
                if pair < 4:
                    v = block(2 * pair + 1)
                    v = v + pltpu.roll(v, 64, 1)
                    u = jnp.where(lane8, u, v)
                else:
                    u = jnp.where(lane8, u, 0.0)
                out_ref[pl.ds(row * 64 + i * 8, 8), :] = u
                row += 1
        return 0
    lax.fori_loop(0, 8, group, 0)
    row = 0
    for j in range(8):
        row += 5 - j // 2
        dr = jnp.zeros((1, 128), F32)
        for q in range(9):
            g = prod_s[q, pl.ds(192, 8), :]
            dr = dr + (g[0:1] + g[1:2]) * coef_s[0, j, pl.ds(q, 1), :]
        dr = dr + pltpu.roll(dr, 64, 1)
        at = (row - 1) * 64
        old = out_ref[pl.ds(at, 8), :]
        keep = lane8 | (lax.broadcasted_iota(jnp.int32, (8, 128), 0) > 0)
        out_ref[pl.ds(at, 8), :] = jnp.where(keep, old, jnp.broadcast_to(dr, (8, 128)))


def reduce_kernel(in_ref, out_ref, from_core, acc_s, from_plane, from_line, send1, recv1, send2, recv2, send3, recv3, send4, recv4, send5, recv5):
    tile = lax.axis_index("tile")
    band = lax.axis_index("band")
    x, z, y, core = tile // 8, tile % 8, band // 2, band % 2

    def dev(xx, yy, zz, cc):
        return (xx * 8 + zz, yy * 2 + cc)

    def plane(e):
        return (x + e // 4) % 4, (y + e % 4) % 4

    order = sorted(range(1, 16), key=lambda e: -(min(e // 4, 4 - e // 4) + min(e % 4, 4 - e % 4)))
    sibling = dev(x, y, z, 1 - core)
    partners = [sibling]
    for e in range(1, 16):
        xx, yy = plane(e)
        partners.append(dev(xx, yy, z, core))
    for e in range(1, 8):
        partners.append(dev(x, y, (z + e) % 8, core))
    barrier = pltpu.get_barrier_semaphore()
    for d in partners:
        pl.semaphore_signal(barrier, inc=1, device_id=d, device_id_type=pl.DeviceIdType.MESH)
    pl.semaphore_wait(barrier, len(partners))

    def copy(src, dst, ss, rs, d):
        return pltpu.make_async_remote_copy(src_ref=src, dst_ref=dst, send_sem=ss, recv_sem=rs, device_id=d,
                                            device_id_type=pl.DeviceIdType.MESH)

    mine = core * HALF
    other = (1 - core) * HALF
    part = HALF // 4
    step1 = []
    for i in range(4):
        c = copy(in_ref.at[pl.ds(pl.multiple_of(other + i * part, 8), part)], from_core.at[pl.ds(i * part, part)],
                 send1.at[i], recv1.at[i], sibling)
        c.start()
        step1.append(c)
    for i in range(4):
        step1[i].wait_recv()
        acc_s[pl.ds(i * part, part), :] = in_ref[pl.ds(pl.multiple_of(mine + i * part, 8), part), :] + from_core[pl.ds(i * part, part), :]

    place = x * 4 + y
    step2 = []
    for e in order:
        xx, yy = plane(e)
        c = copy(acc_s.at[pl.ds(pl.multiple_of((xx * 4 + yy) * PIECE, 8), PIECE)], from_plane.at[e],
                 send2.at[e], recv2.at[e], dev(xx, yy, z, core))
        c.start()
        step2.append(c)
    total = acc_s[pl.ds(pl.multiple_of(place * PIECE, 8), PIECE), :]
    for e, c in zip(order, step2):
        c.wait_recv()
        total = total + from_plane[e]
    from_line[z] = total

    step3 = []
    for e in (4, 3, 5, 2, 6, 1, 7):
        c = copy(from_line.at[z], from_line.at[z], send3.at[e], recv3.at[e], dev(x, y, (z + e) % 8, core))
        c.start()
        step3.append(c)
    for c in step3:
        c.wait_recv()
    total = from_line[0]
    for e in range(1, 8):
        total = total + from_line[e]
    at = pl.multiple_of(mine + place * PIECE, 8)
    out_ref[pl.ds(at, PIECE), :] = total

    step4 = []
    for e in order:
        xx, yy = plane(e)
        c = copy(out_ref.at[pl.ds(at, PIECE)], out_ref.at[pl.ds(at, PIECE)], send4.at[e], recv4.at[e], dev(xx, yy, z, core))
        c.start()
        step4.append(c)
    step5 = []
    c = copy(out_ref.at[pl.ds(at, PIECE)], out_ref.at[pl.ds(at, PIECE)], send5.at[0], recv5.at[0], sibling)
    c.start()
    step5.append(c)
    for e, c4 in reversed(list(zip(order, step4))):
        c4.wait_recv()
        xx, yy = (x + 4 - e // 4) % 4, (y + 4 - e % 4) % 4
        here = pl.multiple_of(mine + (xx * 4 + yy) * PIECE, 8)
        c = copy(out_ref.at[pl.ds(here, PIECE)], out_ref.at[pl.ds(here, PIECE)], send5.at[e], recv5.at[e], sibling)
        c.start()
        step5.append(c)
    for c in step5:
        c.wait_recv()
    for c in step1 + step2 + step3 + step4 + step5:
        c.wait_send()


def dot(a, b, dims=(((1,), (0,)), ((), ()))):
    return lax.dot_general(a, b, dims, precision=lax.Precision.HIGHEST, preferred_element_type=F32)

def invert(m):
    lane = lax.broadcasted_iota(jnp.int32, (8, 128), 1)
    sub = lax.broadcasted_iota(jnp.int32, (8, 128), 0)
    def col(v, c):
        return jnp.broadcast_to(v[:, c:c + 1], (8, 128))
    def rowb(v, c):
        return jnp.broadcast_to(v[c:c + 1, :], (8, 128))
    for p in range(16):
        b = m[p]
        v = [col(b, 8 * p + c) for c in range(8)]
        for c in range(8):
            d = 1.0 / rowb(v[c], c)
            here = sub == c
            for e in range(c + 1, 8):
                r = rowb(v[e], c)
                v[e] = jnp.where(here, v[e] * d, v[e] - (v[c] * r) * d)
            at = lane == 8 * p + c
            r = jnp.where(at, 1.0, rowb(b, c)) * d
            b = jnp.where(here, r, jnp.where(at, 0.0, b) - v[c] * r)
        rows = [rowb(b, c) for c in range(8)]
        panel = (lane >= 8 * p) & (lane < 8 * p + 8)
        order = [i % 16 for i in range(p + 1, p + 16)]
        new = list(m)
        new[p] = b
        for i in order:
            terms = [col(m[i], 8 * p + c) * rows[c] for c in range(8)]
            while len(terms) > 1:
                terms = [x + y for x, y in zip(terms[::2], terms[1::2])]
            new[i] = jnp.where(panel, 0.0, m[i]) - terms[0]
        m = new
    return m

def solve(red_ref, a_s, w_s):
    lane = lax.broadcasted_iota(jnp.int32, (64, 128), 1)
    sub = lax.broadcasted_iota(jnp.int32, (64, 128), 0)
    row = 0
    for j in range(8):
        for pair in range(j // 2, 5):
            u = red_ref[pl.ds(64 * row, 64), :]
            if pair == j // 2:
                u = jnp.where(lane == sub + 64 * (j % 2), u + 511.0, u)
            if pair == 4:
                r = jnp.broadcast_to(u[0:1, :], (64, 128))
                drive = jnp.sum(jnp.where(lane == sub + 64, r, 0.0), axis=1, keepdims=True)
                u = jnp.where(lane < 64, u, jnp.where(lane == 64, drive, 0.0))
            a_s[pl.ds(64 * j, 64), pl.ds(128 * pair, 128)] = u
            row += 1
    for k in range(4):
        at = 128 * k
        m = [a_s[pl.ds(at + 8 * i, 8), pl.ds(at, 128)] for i in range(16)]
        inv = jnp.concatenate(invert(m), axis=0)
        w = dot(inv, a_s[pl.ds(at, 128), pl.ds(at + 128, 512 - at)])
        w_s[pl.ds(at, 128), pl.ds(at + 128, 512 - at)] = w
        for i in range(k + 1, 4):
            ki = a_s[pl.ds(at, 128), pl.ds(128 * i, 128)]
            a_s[pl.ds(128 * i, 128), pl.ds(128 * i, 640 - 128 * i)] -= dot(
                ki, w[:, 128 * (i - k - 1):], (((0,), (0,)), ((), ())))
    for k in (2, 1, 0):
        at = 128 * k
        w_s[pl.ds(at, 128), pl.ds(512, 128)] -= dot(
            w_s[pl.ds(at, 128), pl.ds(at + 128, 384 - at)], w_s[pl.ds(at + 128, 384 - at), pl.ds(512, 128)])


def update_kernel(red_ref, modes_ref, mem_hbm, inc_ref, ana_hbm, a_s, w_s, phi_s, u_s, big_s, mem_s, ana_s, load_sem, save_sem):
    load = pltpu.make_async_copy(mem_hbm, mem_s, load_sem)
    load.start()
    solve(red_ref, a_s, w_s)
    shift = lax.rem(128 - lax.axis_index("band") * 16, 128)
    phi = pltpu.roll(modes_ref[...], shift, 1)
    lane = lax.broadcasted_iota(jnp.int32, (8, 128), 1)
    for width in (16, 32, 64):
        phi = jnp.where(lane < width, phi, jnp.where(lane < 2 * width, pltpu.roll(phi, width, 1), 0.0))
    member = lax.broadcasted_iota(jnp.int32, (64, 1024), 0)
    owner = lax.broadcasted_iota(jnp.int32, (64, 1024), 1) // 16
    for j in range(8):
        wide = jnp.concatenate([jnp.broadcast_to(phi[j : j + 1, :], (64, 128))] * 8, axis=1)
        phi_s[pl.ds(64 * j, 64), :] = jnp.where(member == owner, wide, 0.0)
    u_s[...] = dot(w_s[:, 512:640], phi_s[...], (((0,), (0,)), ((), ())))
    level = lax.broadcasted_iota(jnp.int32, (16, 1024), 1) % 16
    own = level == lax.broadcasted_iota(jnp.int32, (16, 1024), 0)

    def spread(k, _):
        row = jnp.broadcast_to(u_s[pl.ds(k, 1), :], (16, 1024))
        big_s[pl.ds(pl.multiple_of(k * 16, 16), 16), :] = jnp.where(own, row, 0.0).astype(BF)
        return 0

    lax.fori_loop(0, 65, spread, 0, unroll=5)
    load.wait()
    saves = []
    for i in range(4):
        cols = pl.ds(512 * i, 512)
        m = mem_s[:, cols]
        r = jnp.dot(big_s[...], m, preferred_element_type=F32)
        ana_s[:, cols] = (m.astype(F32) - r[:1024]).astype(BF)
        inc_ref[:, cols] = r[1024:]
        save = pltpu.make_async_copy(ana_s.at[:, cols], ana_hbm.at[:, cols], save_sem.at[i])
        save.start()
        saves.append(save)
    for save in saves:
        save.wait()


def per_device(members, modes, *obs):
    def beside(a, forward):
        count = lax.axis_size("band")
        pairs = [(i, i + 1) if forward else (i + 1, i) for i in range(count - 1)]
        return lax.ppermute(a, "band", pairs)

    lo = beside(members[:, 15, :], True)
    hi = beside(members[:, 0, :], False)
    obs = [o.reshape(64, 128) for o in obs]
    field = pl.pallas_call(
        scatter_kernel,
        out_shape=jax.ShapeDtypeStruct((864, 256), F32),
        in_specs=[VM] * 6,
        out_specs=VM,
        scratch_shapes=[pltpu.VMEM((864, 1024), BF), pltpu.VMEM((256, 1024), BF)],
        compiler_params=pltpu.CompilerParams(vmem_limit_bytes=32 * 2**20),
        cost_estimate=pl.CostEstimate(flops=8 * 10**9, bytes_accessed=2**20, transcendentals=0),
        name="scatter",
    )(*obs)
    part = pl.pallas_call(
        sums_kernel,
        out_shape=jax.ShapeDtypeStruct((ROWS, 128), F32),
        in_specs=[VM] * 4 + [pl.BlockSpec(memory_space=pltpu.SMEM)],
        out_specs=VM,
        scratch_shapes=[
            pltpu.VMEM((16, 1024, 128), F32),
            pltpu.VMEM((544, 2048), BF),
            pltpu.VMEM((9, 208, 128), F32),
            pltpu.VMEM((3, 9, 9, 128), F32),
        ],
        compiler_params=pltpu.CompilerParams(vmem_limit_bytes=48 * 2**20),
        name="sums",
    )(field, members, lo, hi, modes)
    red = pl.pallas_call(
        reduce_kernel,
        out_shape=jax.ShapeDtypeStruct((ROWS, 128), F32),
        in_specs=[VM],
        out_specs=VM,
        scratch_shapes=[
            pltpu.VMEM((HALF, 128), F32),
            pltpu.VMEM((HALF, 128), F32),
            pltpu.VMEM((16, PIECE, 128), F32),
            pltpu.VMEM((8, PIECE, 128), F32),
        ]
        + [pltpu.SemaphoreType.DMA((n,)) for n in (4, 4, 16, 16, 8, 8, 16, 16, 16, 16)],
        compiler_params=pltpu.CompilerParams(
            collective_id=0, has_side_effects=True, vmem_limit_bytes=32 * 2**20
        ),
        name="reduce",
    )(part)
    inc, ana = pl.pallas_call(
        update_kernel,
        out_shape=(jax.ShapeDtypeStruct((16, 2048), F32), jax.ShapeDtypeStruct((1024, 2048), BF)),
        in_specs=[VM, VM, pl.BlockSpec(memory_space=pl.ANY)],
        out_specs=(VM, pl.BlockSpec(memory_space=pl.ANY)),
        scratch_shapes=[
            pltpu.VMEM((512, 640), F32),
            pltpu.VMEM((512, 640), F32),
            pltpu.VMEM((512, 1024), F32),
            pltpu.VMEM((128, 1024), F32),
            pltpu.VMEM((1040, 1024), BF),
            pltpu.VMEM((1024, 2048), BF),
            pltpu.VMEM((1024, 2048), BF),
            pltpu.SemaphoreType.DMA,
            pltpu.SemaphoreType.DMA((4,)),
        ],
        compiler_params=pltpu.CompilerParams(vmem_limit_bytes=48 * 2**20),
        name="update",
    )(red, modes, members.reshape(1024, 2048))
    return inc, ana.reshape(64, 16, 2048)


def solution(mesh):
    placed = (
        P(None, "band", "tile"),
        P(),
        P(("tile", "band")),
        P(("tile", "band")),
        P(("tile", "band")),
        P(("tile", "band")),
        P(("tile", "band")),
        P(("tile", "band")),
    )
    return jax.shard_map(
        per_device,
        mesh=mesh,
        in_specs=placed,
        out_specs=(P("band", "tile"), P(None, "band", "tile")),
        check_vma=False,
    )
```

```python
import jax
import jax.numpy as jnp
from jax import lax
from jax.experimental import pallas as pl
from jax.experimental.pallas import tpu as pltpu
from jax.sharding import PartitionSpec as P

BF = jnp.bfloat16
F32 = jnp.float32
VM = pl.BlockSpec(memory_space=pltpu.VMEM)
NT = (((1,), (1,)), ((), ()))
STRIDE = 24
ROWS = 1536
HALF = ROWS // 2
PART = HALF // 2
PIECE = PART // 16


def convert(mem_s, x32_s):
    def conv(m, _):
        v = mem_s[pl.ds(pl.multiple_of(m * 16, 16), 16), :].astype(F32)
        for k in range(16):
            x32_s[k, pl.ds(pl.multiple_of(m * STRIDE + 8, 8), 16), :] = v[:, 128 * k : 128 * k + 128]
        return 0
    lax.fori_loop(0, 64, conv, 0, unroll=2)


def scatter(obs_s, first, field_s, lhs_s, hot_s):
    cell_s, level_s, side_s, weight_s, scale_s, innov_s = obs_s
    rows16 = lax.broadcasted_iota(jnp.int32, (16, 128), 0).astype(F32)
    zero = jnp.zeros((16, 128), BF)
    one = jnp.ones((16, 128), BF)

    def split(v):
        hi = v.astype(BF).astype(F32)
        return hi, v - hi

    def fill(i, slot):
        sl = pl.ds(pl.multiple_of(i * 8, 8), 8)
        cell = cell_s[sl, :]
        lev = level_s[sl, :]
        side = side_s[sl, :]
        w = weight_s[sl, :]
        s = scale_s[sl, :]
        ch = cell >> 8
        keys = [
            (cell & 255).astype(F32),
            ((lev + 1) * 8 + ch).astype(F32),
            ((lev + 2 * side) * 8 + ch).astype(F32),
            ((lev + side + 1) * 8 + ch).astype(F32),
        ]
        a = s * (1.0 - w)
        b = s * w
        t = s * innov_s[sl, :]
        vals = [x for v in (a * a, b * b, a * b, a * t, b * t) for x in split(v)]
        for k in range(8):
            cols = slice(128 * k, 128 * k + 128)

            def wide(v):
                return jnp.broadcast_to(v[k : k + 1, :], (16, 128)).astype(BF)

            cl, kn, kf, kp = [wide(v) for v in keys]
            dn0, dn1, df0, df1, e0, e1, gn0, gn1, gf0, gf1 = [wide(v) for v in vals]
            for g in range(10):
                it = (rows16 + 16.0 * g).astype(BF)
                at = 16 * g
                if g < 9:
                    mn = it == kn
                    mf = it == kf
                    lhs_s[slot, pl.ds(at, 16), cols] = jnp.where(mn, dn0, jnp.where(mf, df0, zero))
                    lhs_s[slot, pl.ds(144 + at, 16), cols] = jnp.where(mn, dn1, jnp.where(mf, df1, zero))
                    lhs_s[slot, pl.ds(288 + at, 16), cols] = jnp.where(mn, gn0, jnp.where(mf, gf0, zero))
                    lhs_s[slot, pl.ds(432 + at, 16), cols] = jnp.where(mn, gn1, jnp.where(mf, gf1, zero))
                mp = it == kp
                lhs_s[slot, pl.ds(576 + at, 16), cols] = jnp.where(mp, e0, zero)
                lhs_s[slot, pl.ds(736 + at, 16), cols] = jnp.where(mp, e1, zero)
            for g in range(16):
                it = (rows16 + 16.0 * g).astype(BF)
                hot_s[slot, pl.ds(16 * g, 16), cols] = jnp.where(it == cl, one, zero)

    def add(slot):
        field_s[...] += lax.dot_general(lhs_s[slot], hot_s[slot], NT, preferred_element_type=F32)

    fill(first, 0)

    def steps(i, _):
        at = first + 2 * i
        fill(at + 1, 1)
        add(0)
        fill(at + 2, 0)
        add(1)
        return 0

    lax.fori_loop(0, 1, steps, 0)
    fill(first + 3, 1)
    add(0)
    add(1)


def products(field_s, x32_s, stack_s, prod_s):
    first = lax.broadcasted_iota(jnp.int32, (16, 128), 0)
    lane = lax.broadcasted_iota(jnp.int32, (144, 128), 1)

    def field(base, step, r):
        at = pl.multiple_of(base + 8 * r, 8)
        return field_s[pl.ds(at, 8), :] + field_s[pl.ds(pl.multiple_of(at + step, 8), 8), :]

    def fill(q, slot):
        r = 2 * q
        below = jnp.maximum(r - 1, 0)
        ed = [field(576, 160, r + i) for i in range(2)]
        dd = [field(0, 144, r + i) for i in range(2)]
        gd = [field(288, 144, r + i) for i in range(2)]
        for k in range(16):
            cs = slice(128 * k, 128 * k + 128)

            def row(v):
                return v[k // 2 : k // 2 + 1, 128 * (k % 2) : 128 * (k % 2) + 128]

            xs = [x32_s[k, pl.ds(7 + l, 64, stride=STRIDE), :] for l in (below, r, r + 1)]
            for h in range(2):
                base = 144 * h
                stack_s[slot, pl.ds(288 + 64 * h, 64), cs] = xs[h + 1].astype(BF)
                stack_s[slot, pl.ds(base, 64), cs] = (xs[h + 1] * row(dd[h])).astype(BF)
                stack_s[slot, pl.ds(base + 64, 64), cs] = (xs[h] * row(ed[h])).astype(BF)
                g = jnp.broadcast_to(row(gd[h]), (16, 128))
                gh = g.astype(BF).astype(F32)
                both = jnp.where(first == 0, gh, jnp.where(first == 1, g - gh, 0.0))
                stack_s[slot, pl.ds(base + 128, 16), cs] = both.astype(BF)

    def multiply(q, slot):
        p = lax.dot_general(
            stack_s[slot, pl.ds(0, 288), :], stack_s[slot, pl.ds(288, 128), :], NT, preferred_element_type=F32
        )
        prod_s[q] = jnp.where(lane < 64, p[:144], p[144:])

    fill(0, 0)

    def steps(i, _):
        fill(2 * i + 1, 1)
        multiply(2 * i, 0)
        fill(2 * i + 2, 0)
        multiply(2 * i + 1, 1)
        return 0

    lax.fori_loop(0, 4, steps, 0)
    multiply(8, 0)


def coefs(modes_ref, start, coef_s):
    half = lax.broadcasted_iota(jnp.int32, (1, 128), 1) < 64
    for j in range(9):
        if j < 8:
            phi = []
            for r in range(-1, 19):
                l = start + r
                ok = (l >= 0) & (l < 128)
                phi.append(jnp.where(ok, modes_ref[j, jnp.clip(l, 0, 127)], 0.0))
        else:
            phi = [jnp.float32(1.0)] * 20
        for q in range(9):
            for s in range(3):
                r = 2 * q + (1, 0, 2)[s]
                coef_s[s, j, pl.ds(q, 1), :] = jnp.where(half, phi[r], phi[r + 1])


HALVES = [(j, jj) for j in range(8) for jj in range(j, 9)]


def expand(prod_s, above_s, coef_s, out_ref):
    left64 = lax.broadcasted_iota(jnp.int32, (64, 128), 1) < 64

    def transpose(q, _):
        above = jnp.minimum(q + 1, 8)
        t = jnp.concatenate([prod_s[q, pl.ds(64, 64), :], prod_s[above, pl.ds(64, 64), :]], axis=0).T
        right = jnp.where(q < 8, t[:64], 0.0)
        above_s[q] = jnp.where(left64, t[64:], right)
        return 0

    lax.fori_loop(0, 9, transpose, 0)
    lane8 = lax.broadcasted_iota(jnp.int32, (8, 128), 1) < 64

    def group(i, _):
        at = pl.multiple_of(i * 8, 8)
        s0 = [prod_s[q, pl.ds(at, 8), :] for q in range(9)]
        s1 = [prod_s[q, pl.ds(pl.multiple_of(64 + at, 8), 8), :] for q in range(9)]
        s2 = [above_s[q, pl.ds(at, 8), :] for q in range(9)]
        held, t = None, None
        for n, (j, jj) in enumerate(HALVES):
            if jj == j:
                t = [
                    s0[q] * coef_s[0, j, pl.ds(q, 1), :]
                    + s1[q] * coef_s[1, j, pl.ds(q, 1), :]
                    + s2[q] * coef_s[2, j, pl.ds(q, 1), :]
                    for q in range(9)
                ]
            acc = t[0] * coef_s[0, jj, pl.ds(0, 1), :]
            for q in range(1, 9):
                acc = acc + t[q] * coef_s[0, jj, pl.ds(q, 1), :]
            acc = acc + pltpu.roll(acc, 64, 1)
            if n % 2 == 0:
                held = acc
            else:
                out_ref[pl.ds(pl.multiple_of(n // 2 * 64 + at, 8), 8), :] = jnp.where(lane8, held, acc)
        return 0

    lax.fori_loop(0, 8, group, 0)
    out_ref[pl.ds(1408, 128), :] = jnp.zeros((128, 128), F32)
    for j in range(8):
        dr = jnp.zeros((1, 128), F32)
        for q in range(9):
            g = prod_s[q, pl.ds(128, 8), :]
            dr = dr + (g[0:1] + g[1:2]) * coef_s[0, j, pl.ds(q, 1), :]
        out_ref[pl.ds(1408 + j, 1), :] = dr + pltpu.roll(dr, 64, 1)


def front_kernel(
    cell_h, level_h, side_h, weight_h, scale_h, innov_h, mem_h, modes_ref, out_ref,
    cell_s, level_s, side_s, weight_s, scale_s, innov_s, mem_s, lhs_s, hot_s, field_s, x32_s, stack_s, prod_s, above_s,
    coef_s, edge_s, halo_s, part_s, from_core, acc_s, from_plane, from_line,
    obs_sem, mem_sem, send0, recv0, send1, recv1, send2, recv2, send3, recv3, send4, recv4, send5, recv5,
):
    tile = lax.axis_index("tile")
    band = lax.axis_index("band")
    x, z, y, core = tile // 8, tile % 8, band // 2, band % 2

    def dev(xx, yy, zz, cc):
        return (xx * 8 + zz, yy * 2 + cc)

    def plane(e):
        return (x + e // 4) % 4, (y + e % 4) % 4

    order = sorted(range(1, 16), key=lambda e: -(min(e // 4, 4 - e // 4) + min(e % 4, 4 - e % 4)))
    sibling = dev(x, y, z, 1 - core)
    up = (tile, (band + 1) % 8)
    down = (tile, (band + 7) % 8)
    partners = [up, down]
    for e in range(1, 16):
        partners.append(dev(*plane(e), z, core))
    for e in range(1, 8):
        partners.append(dev(x, y, (z + e) % 8, core))
    barrier = pltpu.get_barrier_semaphore()
    for d in partners:
        pl.semaphore_signal(barrier, inc=1, device_id=d, device_id_type=pl.DeviceIdType.MESH)

    obs_s = (cell_s, level_s, side_s, weight_s, scale_s, innov_s)
    loads = []
    for n, (h, s) in enumerate(zip((cell_h, level_h, side_h, weight_h, scale_h, innov_h), obs_s)):
        c = pltpu.make_async_copy(h, s, obs_sem.at[n])
        c.start()
        loads.append(c)
    mem_load = pltpu.make_async_copy(mem_h, mem_s, mem_sem)
    mem_load.start()
    coefs(modes_ref, band * 16 - 1, coef_s)
    field_s[...] = jnp.zeros_like(field_s)
    for c in loads:
        c.wait()
    scatter(obs_s, 0, field_s, lhs_s, hot_s)
    mem_load.wait()
    convert(mem_s, x32_s)
    for k in range(16):
        cs = slice(128 * k, 128 * k + 128)
        edge_s[0, :, cs] = x32_s[k, pl.ds(8, 64, stride=STRIDE), :].astype(BF)
        edge_s[1, :, cs] = x32_s[k, pl.ds(23, 64, stride=STRIDE), :].astype(BF)
    pl.semaphore_wait(barrier, len(partners))

    def copy(src, dst, ss, rs, d):
        c = pltpu.make_async_remote_copy(
            src_ref=src, dst_ref=dst, send_sem=ss, recv_sem=rs, device_id=d, device_id_type=pl.DeviceIdType.MESH
        )
        c.start()
        return c

    halo = [
        copy(edge_s.at[0], halo_s.at[1], send0.at[0], recv0.at[0], down),
        copy(edge_s.at[1], halo_s.at[0], send0.at[1], recv0.at[1], up),
    ]
    scatter(obs_s, 4, field_s, lhs_s, hot_s)
    for c in halo:
        c.wait()
    for k in range(16):
        cs = slice(128 * k, 128 * k + 128)
        x32_s[k, pl.ds(7, 64, stride=STRIDE), :] = jnp.where(band > 0, halo_s[0, :, cs].astype(F32), 0.0)
        x32_s[k, pl.ds(24, 64, stride=STRIDE), :] = jnp.where(band < 7, halo_s[1, :, cs].astype(F32), 0.0)
    products(field_s, x32_s, stack_s, prod_s)
    expand(prod_s, above_s, coef_s, part_s)

    mine = core * HALF
    other = (1 - core) * HALF
    place = x * 4 + y

    def rows(base, at, n):
        return pl.ds(pl.multiple_of(base + at, 8), n)

    step1, step2, step3, step4, step5 = [], [], [], [], []
    for i in range(2):
        step1.append(
            copy(part_s.at[rows(other, i * PART, PART)], from_core.at[pl.ds(i * PART, PART)], send1.at[i], recv1.at[i], sibling)
        )
    for i in range(2):
        step1[i].wait_recv()
        acc_s[pl.ds(i * PART, PART), :] = part_s[rows(mine, i * PART, PART), :] + from_core[pl.ds(i * PART, PART), :]
        for e in order:
            xx, yy = plane(e)
            src = acc_s.at[rows((xx * 4 + yy) * PIECE, i * PART, PIECE)]
            step2.append(copy(src, from_plane.at[i, e], send2.at[i, e], recv2.at[i, e], dev(xx, yy, z, core)))
    for i in range(2):
        total = acc_s[rows(place * PIECE, i * PART, PIECE), :]
        for n, e in enumerate(order):
            step2[15 * i + n].wait_recv()
            total = total + from_plane[i, e]
        from_line[i, z] = total
        for e in (4, 3, 5, 2, 6, 1, 7):
            ref = from_line.at[i, z]
            step3.append(copy(ref, ref, send3.at[i, e], recv3.at[i, e], dev(x, y, (z + e) % 8, core)))
    for i in range(2):
        for c in step3[7 * i : 7 * i + 7]:
            c.wait_recv()
        total = from_line[i, 0]
        for e in range(1, 8):
            total = total + from_line[i, e]
        at = rows(mine, i * PART + place * PIECE, PIECE)
        out_ref[at, :] = total
        ref = out_ref.at[at]
        for e in order:
            step4.append(copy(ref, ref, send4.at[i, e], recv4.at[i, e], dev(*plane(e), z, core)))
        step5.append(copy(ref, ref, send5.at[i, 0], recv5.at[i, 0], sibling))
    for i in range(2):
        for n, e in reversed(list(enumerate(order))):
            step4[15 * i + n].wait_recv()
            xx, yy = (x + 4 - e // 4) % 4, (y + 4 - e % 4) % 4
            ref = out_ref.at[rows(mine, i * PART + (xx * 4 + yy) * PIECE, PIECE)]
            step5.append(copy(ref, ref, send5.at[i, e], recv5.at[i, e], sibling))
    for c in step5:
        c.wait_recv()
    for c in step1 + step2 + step3 + step4 + step5:
        c.wait_send()


def dot(a, b, dims=(((1,), (0,)), ((), ()))):
    return lax.dot_general(a, b, dims, precision=lax.Precision.HIGHEST, preferred_element_type=F32)


def invert(m):
    lane = lax.broadcasted_iota(jnp.int32, (8, 128), 1)
    sub = lax.broadcasted_iota(jnp.int32, (8, 128), 0)
    def col(v, c):
        return jnp.broadcast_to(v[:, c:c + 1], (8, 128))
    def rowb(v, c):
        return jnp.broadcast_to(v[c:c + 1, :], (8, 128))
    for p in range(16):
        b = m[p]
        v = [col(b, 8 * p + c) for c in range(8)]
        for c in range(8):
            d = 1.0 / rowb(v[c], c)
            here = sub == c
            for e in range(c + 1, 8):
                r = rowb(v[e], c)
                v[e] = jnp.where(here, v[e] * d, v[e] - (v[c] * r) * d)
            at = lane == 8 * p + c
            r = jnp.where(at, 1.0, rowb(b, c)) * d
            b = jnp.where(here, r, jnp.where(at, 0.0, b) - v[c] * r)
        rows = [rowb(b, c) for c in range(8)]
        panel = (lane >= 8 * p) & (lane < 8 * p + 8)
        order = [i % 16 for i in range(p + 1, p + 16)]
        new = list(m)
        new[p] = b
        for i in order:
            terms = [col(m[i], 8 * p + c) * rows[c] for c in range(8)]
            while len(terms) > 1:
                terms = [x + y for x, y in zip(terms[::2], terms[1::2])]
            new[i] = jnp.where(panel, 0.0, m[i]) - terms[0]
        m = new
    return m

def solve(red_ref, a_s, w_s):
    lane = lax.broadcasted_iota(jnp.int32, (64, 128), 1)
    sub = lax.broadcasted_iota(jnp.int32, (64, 128), 0)
    where = {pair: n for n, pair in enumerate(HALVES)}

    def half(j, jj, side):
        n = where[j, jj]
        v = red_ref[pl.ds(64 * (n // 2), 64), :]
        return v if n % 2 == side else pltpu.roll(v, 64, 1)

    for j in range(8):
        for pair in range(j // 2, 5):
            if pair == 4:
                r = jnp.broadcast_to(red_ref[pl.ds(1408 + j, 1), :], (64, 128))
                drive = jnp.sum(jnp.where(lane == sub, r, 0.0), axis=1, keepdims=True)
                u = jnp.where(lane < 64, half(j, 8, 0), jnp.where(lane == 64, drive, 0.0))
            elif 2 * pair < j:
                t = a_s[pl.ds(64 * j - 64, 64), pl.ds(128 * pair, 128)]
                t = jnp.concatenate([t, t], axis=0).T[64:]
                u = jnp.where(lane < 64, t, half(j, j, 1))
            else:
                u = jnp.where(lane < 64, half(j, 2 * pair, 0), half(j, 2 * pair + 1, 1))
            if pair == j // 2:
                u = jnp.where(lane == sub + 64 * (j % 2), u + 511.0, u)
            a_s[pl.ds(64 * j, 64), pl.ds(128 * pair, 128)] = u
    for k in range(4):
        at = 128 * k
        m = [a_s[pl.ds(at + 8 * i, 8), pl.ds(at, 128)] for i in range(16)]
        inv = jnp.concatenate(invert(m), axis=0)
        w = dot(inv, a_s[pl.ds(at, 128), pl.ds(at + 128, 512 - at)])
        w_s[pl.ds(at, 128), pl.ds(at + 128, 512 - at)] = w
        for i in range(k + 1, 4):
            ki = a_s[pl.ds(at, 128), pl.ds(128 * i, 128)]
            a_s[pl.ds(128 * i, 128), pl.ds(128 * i, 640 - 128 * i)] -= dot(
                ki, w[:, 128 * (i - k - 1):], (((0,), (0,)), ((), ())))
    for k in (2, 1, 0):
        at = 128 * k
        w_s[pl.ds(at, 128), pl.ds(512, 128)] -= dot(
            w_s[pl.ds(at, 128), pl.ds(at + 128, 384 - at)], w_s[pl.ds(at + 128, 384 - at), pl.ds(512, 128)])


def update_kernel(red_ref, modes_ref, mem_hbm, inc_ref, ana_hbm, a_s, w_s, phi_s, u_s, big_s, mem_s, ana_s, load_sem, save_sem):
    load = pltpu.make_async_copy(mem_hbm, mem_s, load_sem)
    load.start()
    solve(red_ref, a_s, w_s)
    shift = lax.rem(128 - lax.axis_index("band") * 16, 128)
    phi = pltpu.roll(modes_ref[...], shift, 1)
    lane = lax.broadcasted_iota(jnp.int32, (8, 128), 1)
    for width in (16, 32, 64):
        phi = jnp.where(lane < width, phi, jnp.where(lane < 2 * width, pltpu.roll(phi, width, 1), 0.0))
    member = lax.broadcasted_iota(jnp.int32, (64, 1024), 0)
    owner = lax.broadcasted_iota(jnp.int32, (64, 1024), 1) // 16
    for j in range(8):
        wide = jnp.concatenate([jnp.broadcast_to(phi[j : j + 1, :], (64, 128))] * 8, axis=1)
        phi_s[pl.ds(64 * j, 64), :] = jnp.where(member == owner, wide, 0.0)
    u_s[...] = dot(w_s[:, 512:640], phi_s[...], (((0,), (0,)), ((), ())))
    level = lax.broadcasted_iota(jnp.int32, (16, 1024), 1) % 16
    own = level == lax.broadcasted_iota(jnp.int32, (16, 1024), 0)

    def spread(k, _):
        row = jnp.broadcast_to(u_s[pl.ds(k, 1), :], (16, 1024))
        big_s[pl.ds(pl.multiple_of(k * 16, 16), 16), :] = jnp.where(own, row, 0.0).astype(BF)
        return 0

    lax.fori_loop(0, 65, spread, 0, unroll=5)
    load.wait()
    saves = []
    for i in range(4):
        cols = pl.ds(512 * i, 512)
        m = mem_s[:, cols]
        r = jnp.dot(big_s[...], m, preferred_element_type=F32)
        ana_s[:, cols] = (m.astype(F32) - r[:1024]).astype(BF)
        inc_ref[:, cols] = r[1024:]
        save = pltpu.make_async_copy(ana_s.at[:, cols], ana_hbm.at[:, cols], save_sem.at[i])
        save.start()
        saves.append(save)
    for save in saves:
        save.wait()


def per_device(members, modes, *obs):
    flat = members.reshape(1024, 2048)
    anywhere = pl.BlockSpec(memory_space=pl.ANY)
    red = pl.pallas_call(
        front_kernel,
        out_shape=jax.ShapeDtypeStruct((ROWS, 128), F32),
        in_specs=[anywhere] * 7 + [pl.BlockSpec(memory_space=pltpu.SMEM)],
        out_specs=VM,
        scratch_shapes=[pltpu.VMEM((64, 128), jnp.int32)] * 3
        + [pltpu.VMEM((64, 128), F32)] * 3
        + [
            pltpu.VMEM((1024, 2048), BF),
            pltpu.VMEM((2, 896, 1024), BF),
            pltpu.VMEM((2, 256, 1024), BF),
            pltpu.VMEM((896, 256), F32),
            pltpu.VMEM((16, 64 * STRIDE + 8, 128), F32),
            pltpu.VMEM((2, 416, 2048), BF),
            pltpu.VMEM((9, 144, 128), F32),
            pltpu.VMEM((9, 64, 128), F32),
            pltpu.VMEM((3, 9, 9, 128), F32),
            pltpu.VMEM((2, 64, 2048), BF),
            pltpu.VMEM((2, 64, 2048), BF),
            pltpu.VMEM((ROWS, 128), F32),
            pltpu.VMEM((HALF, 128), F32),
            pltpu.VMEM((HALF, 128), F32),
            pltpu.VMEM((2, 16, PIECE, 128), F32),
            pltpu.VMEM((2, 8, PIECE, 128), F32),
            pltpu.SemaphoreType.DMA((6,)),
            pltpu.SemaphoreType.DMA,
        ]
        + [pltpu.SemaphoreType.DMA(n) for n in ((2,), (2,), (2,), (2,))]
        + [pltpu.SemaphoreType.DMA((2, n)) for n in (16, 16, 8, 8, 16, 16, 16, 16)],
        compiler_params=pltpu.CompilerParams(
            collective_id=0, has_side_effects=True, vmem_limit_bytes=56 * 2**20
        ),
        name="front",
    )(*[o.reshape(64, 128) for o in obs], flat, modes)
    inc, ana = pl.pallas_call(
        update_kernel,
        out_shape=(jax.ShapeDtypeStruct((16, 2048), F32), jax.ShapeDtypeStruct((1024, 2048), BF)),
        in_specs=[VM, VM, anywhere],
        out_specs=(VM, anywhere),
        scratch_shapes=[
            pltpu.VMEM((512, 640), F32),
            pltpu.VMEM((512, 640), F32),
            pltpu.VMEM((512, 1024), F32),
            pltpu.VMEM((128, 1024), F32),
            pltpu.VMEM((1040, 1024), BF),
            pltpu.VMEM((1024, 2048), BF),
            pltpu.VMEM((1024, 2048), BF),
            pltpu.SemaphoreType.DMA,
            pltpu.SemaphoreType.DMA((4,)),
        ],
        compiler_params=pltpu.CompilerParams(vmem_limit_bytes=48 * 2**20),
        name="update",
    )(red, modes, flat)
    return inc, ana.reshape(64, 16, 2048)


def solution(mesh):
    placed = (
        P(None, "band", "tile"),
        P(),
        P(("tile", "band")),
        P(("tile", "band")),
        P(("tile", "band")),
        P(("tile", "band")),
        P(("tile", "band")),
        P(("tile", "band")),
    )
    return jax.shard_map(
        per_device,
        mesh=mesh,
        in_specs=placed,
        out_specs=(P("band", "tile"), P(None, "band", "tile")),
        check_vma=False,
    )
```

```python
import jax
import jax.numpy as jnp
from jax import lax
from jax.experimental import pallas as pl
from jax.experimental.pallas import tpu as pltpu
from jax.sharding import PartitionSpec as P

BF = jnp.bfloat16
F32 = jnp.float32
VM = pl.BlockSpec(memory_space=pltpu.VMEM)
NT = (((1,), (1,)), ((), ()))
STRIDE = 24
ROWS = 1536
PART = ROWS // 4
PIECE = PART // 16


def convert(mem_s, x32_s):
    def conv(m, _):
        v = mem_s[pl.ds(pl.multiple_of(m * 16, 16), 16), :].astype(F32)
        for k in range(16):
            x32_s[k, pl.ds(pl.multiple_of(m * STRIDE + 8, 8), 16), :] = v[:, 128 * k : 128 * k + 128]
        return 0
    lax.fori_loop(0, 64, conv, 0, unroll=2)


def scatter(obs_s, field_s, lhs_s, hot_s):
    cell_s, level_s, side_s, weight_s, scale_s, innov_s = obs_s
    rows16 = lax.broadcasted_iota(jnp.int32, (16, 128), 0).astype(F32)
    zero = jnp.zeros((16, 128), BF)
    one = jnp.ones((16, 128), BF)

    def split(v):
        hi = v.astype(BF).astype(F32)
        return hi, v - hi

    def fill(i, slot):
        sl = pl.ds(pl.multiple_of(i * 8, 8), 8)
        cell = cell_s[sl, :]
        lev = level_s[sl, :]
        side = side_s[sl, :]
        w = weight_s[sl, :]
        s = scale_s[sl, :]
        ch = cell >> 8
        keys = [
            (cell & 255).astype(F32),
            ((lev + 1) * 8 + ch).astype(F32),
            ((lev + 2 * side) * 8 + ch).astype(F32),
            ((lev + side + 1) * 8 + ch).astype(F32),
        ]
        a = s * (1.0 - w)
        b = s * w
        t = s * innov_s[sl, :]
        vals = [x for v in (a * a, b * b, a * b, a * t, b * t) for x in split(v)]
        for k in range(8):
            cols = slice(128 * k, 128 * k + 128)

            def wide(v):
                return jnp.broadcast_to(v[k : k + 1, :], (16, 128)).astype(BF)

            cl, kn, kf, kp = [wide(v) for v in keys]
            dn0, dn1, df0, df1, e0, e1, gn0, gn1, gf0, gf1 = [wide(v) for v in vals]
            for g in range(10):
                it = (rows16 + 16.0 * g).astype(BF)
                at = 16 * g
                if g < 9:
                    mn = it == kn
                    mf = it == kf
                    lhs_s[slot, pl.ds(at, 16), cols] = jnp.where(mn, dn0, jnp.where(mf, df0, zero))
                    lhs_s[slot, pl.ds(144 + at, 16), cols] = jnp.where(mn, dn1, jnp.where(mf, df1, zero))
                    lhs_s[slot, pl.ds(288 + at, 16), cols] = jnp.where(mn, gn0, jnp.where(mf, gf0, zero))
                    lhs_s[slot, pl.ds(432 + at, 16), cols] = jnp.where(mn, gn1, jnp.where(mf, gf1, zero))
                mp = it == kp
                lhs_s[slot, pl.ds(576 + at, 16), cols] = jnp.where(mp, e0, zero)
                lhs_s[slot, pl.ds(736 + at, 16), cols] = jnp.where(mp, e1, zero)
            for g in range(16):
                it = (rows16 + 16.0 * g).astype(BF)
                hot_s[slot, pl.ds(16 * g, 16), cols] = jnp.where(it == cl, one, zero)

    def add(slot):
        field_s[...] += lax.dot_general(lhs_s[slot], hot_s[slot], NT, preferred_element_type=F32)

    fill(0, 0)

    def steps(i, _):
        fill(2 * i + 1, 1)
        add(0)
        fill(2 * i + 2, 0)
        add(1)
        return 0

    lax.fori_loop(0, 3, steps, 0)
    fill(7, 1)
    add(0)
    add(1)


def products(ends, field_s, x32_s, stack_s, prod_s):
    first = lax.broadcasted_iota(jnp.int32, (16, 128), 0)
    lane = lax.broadcasted_iota(jnp.int32, (144, 128), 1)

    def field(base, step, r):
        at = pl.multiple_of(base + 8 * r, 8)
        return field_s[pl.ds(at, 8), :] + field_s[pl.ds(pl.multiple_of(at + step, 8), 8), :]

    def fill(q, slot):
        r = 2 * q
        below = jnp.maximum(r - 1, 0)
        ed = [field(576, 160, r + i) for i in range(2)]
        dd = [field(0, 144, r + i) for i in range(2)]
        gd = [field(288, 144, r + i) for i in range(2)]
        for k in range(16):
            cs = slice(128 * k, 128 * k + 128)

            def row(v):
                return v[k // 2 : k // 2 + 1, 128 * (k % 2) : 128 * (k % 2) + 128]

            xs = [x32_s[k, pl.ds(7 + l, 64, stride=STRIDE), :] for l in (below, r, r + 1)]
            for h in range(2):
                base = 144 * h
                stack_s[slot, pl.ds(288 + 64 * h, 64), cs] = xs[h + 1].astype(BF)
                stack_s[slot, pl.ds(base, 64), cs] = (xs[h + 1] * row(dd[h])).astype(BF)
                stack_s[slot, pl.ds(base + 64, 64), cs] = (xs[h] * row(ed[h])).astype(BF)
                g = jnp.broadcast_to(row(gd[h]), (16, 128))
                gh = g.astype(BF).astype(F32)
                both = jnp.where(first == 0, gh, jnp.where(first == 1, g - gh, 0.0))
                stack_s[slot, pl.ds(base + 128, 16), cs] = both.astype(BF)

    def multiply(q, slot):
        p = lax.dot_general(
            stack_s[slot, pl.ds(0, 288), :], stack_s[slot, pl.ds(288, 128), :], NT, preferred_element_type=F32
        )
        prod_s[q] = jnp.where(lane < 64, p[:144], p[144:])

    fill(1, 0)

    def steps(i, _):
        fill(2 * i + 2, 1)
        multiply(2 * i + 1, 0)
        fill(2 * i + 3, 0)
        multiply(2 * i + 2, 1)
        return 0

    lax.fori_loop(0, 3, steps, 0)
    multiply(7, 0)
    ends()
    fill(0, 0)
    fill(8, 1)
    multiply(0, 0)
    multiply(8, 1)


def coefs(modes_ref, start, coef_s):
    half = lax.broadcasted_iota(jnp.int32, (1, 128), 1) < 64
    for j in range(9):
        if j < 8:
            phi = []
            for r in range(-1, 19):
                l = start + r
                ok = (l >= 0) & (l < 128)
                phi.append(jnp.where(ok, modes_ref[j, jnp.clip(l, 0, 127)], 0.0))
        else:
            phi = [jnp.float32(1.0)] * 20
        for q in range(9):
            for s in range(3):
                r = 2 * q + (1, 0, 2)[s]
                coef_s[s, j, pl.ds(q, 1), :] = jnp.where(half, phi[r], phi[r + 1])


HALVES = [(j, jj) for j in range(8) for jj in range(j, 9)]


def levels_above(prod_s, above_s):
    left64 = lax.broadcasted_iota(jnp.int32, (64, 128), 1) < 64

    def transpose(q, _):
        above = jnp.minimum(q + 1, 8)
        t = jnp.concatenate([prod_s[q, pl.ds(64, 64), :], prod_s[above, pl.ds(64, 64), :]], axis=0).T
        right = jnp.where(q < 8, t[:64], 0.0)
        above_s[q] = jnp.where(left64, t[64:], right)
        return 0

    lax.fori_loop(0, 9, transpose, 0)


def expand(part, prod_s, above_s, coef_s, out_ref):
    base = part * 768
    lane8 = lax.broadcasted_iota(jnp.int32, (8, 128), 1) < 64

    def group(i, _):
        at = pl.multiple_of(part * 32 + i * 8, 8)
        s0 = [prod_s[q, pl.ds(at, 8), :] for q in range(9)]
        s1 = [prod_s[q, pl.ds(pl.multiple_of(64 + at, 8), 8), :] for q in range(9)]
        s2 = [above_s[q, pl.ds(at, 8), :] for q in range(9)]
        held, t = None, None
        for n, (j, jj) in enumerate(HALVES):
            if jj == j:
                t = [
                    s0[q] * coef_s[0, j, pl.ds(q, 1), :]
                    + s1[q] * coef_s[1, j, pl.ds(q, 1), :]
                    + s2[q] * coef_s[2, j, pl.ds(q, 1), :]
                    for q in range(9)
                ]
            acc = t[0] * coef_s[0, jj, pl.ds(0, 1), :]
            for q in range(1, 9):
                acc = acc + t[q] * coef_s[0, jj, pl.ds(q, 1), :]
            acc = acc + pltpu.roll(acc, 64, 1)
            if n % 2 == 0:
                held = acc
            else:
                out_ref[pl.ds(pl.multiple_of(base + n // 2 * 32 + i * 8, 8), 8), :] = jnp.where(lane8, held, acc)
        return 0

    lax.fori_loop(0, 4, group, 0)
    out_ref[pl.ds(base + 704, 64), :] = jnp.zeros((64, 128), F32)
    if part > 0:
        return
    for j in range(8):
        dr = jnp.zeros((1, 128), F32)
        for q in range(9):
            g = prod_s[q, pl.ds(128, 8), :]
            dr = dr + (g[0:1] + g[1:2]) * coef_s[0, j, pl.ds(q, 1), :]
        out_ref[pl.ds(704 + j, 1), :] = dr + pltpu.roll(dr, 64, 1)


def front_kernel(
    cell_h, level_h, side_h, weight_h, scale_h, innov_h, mem_h, modes_ref, out_ref,
    cell_s, level_s, side_s, weight_s, scale_s, innov_s, mem_s, lhs_s, hot_s, field_s, x32_s, stack_s, prod_s, above_s,
    coef_s, edge_s, halo_s, part_s, from_core, acc_s, from_plane, from_line,
    obs_sem, mem_sem, send0, recv0, send1, recv1, send2, recv2, send3, recv3, send4, recv4, send5, recv5,
):
    tile = lax.axis_index("tile")
    band = lax.axis_index("band")
    x, z, y, core = tile // 8, tile % 8, band // 2, band % 2

    def dev(xx, yy, zz, cc):
        return (xx * 8 + zz, yy * 2 + cc)

    def plane(e):
        return (x + e // 4) % 4, (y + e % 4) % 4

    order = sorted(range(1, 16), key=lambda e: -(min(e // 4, 4 - e // 4) + min(e % 4, 4 - e % 4)))
    sibling = dev(x, y, z, 1 - core)
    up = (tile, (band + 1) % 8)
    down = (tile, (band + 7) % 8)
    partners = [up, down]
    for e in range(1, 16):
        partners.append(dev(*plane(e), z, core))
    for e in range(1, 8):
        partners.append(dev(x, y, (z + e) % 8, core))
    barrier = pltpu.get_barrier_semaphore()
    for d in partners:
        pl.semaphore_signal(barrier, inc=1, device_id=d, device_id_type=pl.DeviceIdType.MESH)

    obs_s = (cell_s, level_s, side_s, weight_s, scale_s, innov_s)
    loads = []
    for n, (h, s) in enumerate(zip((cell_h, level_h, side_h, weight_h, scale_h, innov_h), obs_s)):
        c = pltpu.make_async_copy(h, s, obs_sem.at[n])
        c.start()
        loads.append(c)
    mem_load = pltpu.make_async_copy(mem_h, mem_s, mem_sem)
    mem_load.start()
    coefs(modes_ref, band * 16 - 1, coef_s)
    field_s[...] = jnp.zeros_like(field_s)
    for c in loads:
        c.wait()
    scatter(obs_s, field_s, lhs_s, hot_s)
    mem_load.wait()
    convert(mem_s, x32_s)
    for k in range(16):
        cs = slice(128 * k, 128 * k + 128)
        edge_s[0, :, cs] = x32_s[k, pl.ds(8, 64, stride=STRIDE), :].astype(BF)
        edge_s[1, :, cs] = x32_s[k, pl.ds(23, 64, stride=STRIDE), :].astype(BF)
    pl.semaphore_wait(barrier, len(partners))

    def copy(src, dst, ss, rs, d):
        c = pltpu.make_async_remote_copy(
            src_ref=src, dst_ref=dst, send_sem=ss, recv_sem=rs, device_id=d, device_id_type=pl.DeviceIdType.MESH
        )
        c.start()
        return c

    halo = [
        copy(edge_s.at[0], halo_s.at[1], send0.at[0], recv0.at[0], down),
        copy(edge_s.at[1], halo_s.at[0], send0.at[1], recv0.at[1], up),
    ]
    def ends():
        for c in halo:
            c.wait()
        for k in range(16):
            cs = slice(128 * k, 128 * k + 128)
            x32_s[k, pl.ds(7, 64, stride=STRIDE), :] = jnp.where(band > 0, halo_s[0, :, cs].astype(F32), 0.0)
            x32_s[k, pl.ds(24, 64, stride=STRIDE), :] = jnp.where(band < 7, halo_s[1, :, cs].astype(F32), 0.0)

    products(ends, field_s, x32_s, stack_s, prod_s)

    place = x * 4 + y

    def rows(i, whose, at, n):
        return pl.ds(pl.multiple_of((2 * i + whose) * PART + at, 8), n)

    step1, step2, step3, step4, step5 = [], [], [], [], []
    levels_above(prod_s, above_s)
    for i in range(2):
        expand(i, prod_s, above_s, coef_s, part_s)
        ref = part_s.at[rows(i, 1 - core, 0, PART)]
        step1.append(copy(ref, from_core.at[i], send1.at[i], recv1.at[i], sibling))
    for i in range(2):
        step1[i].wait_recv()
        acc_s[i] = part_s[rows(i, core, 0, PART), :] + from_core[i]
        for e in order:
            xx, yy = plane(e)
            src = acc_s.at[i, pl.ds(pl.multiple_of((xx * 4 + yy) * PIECE, 8), PIECE)]
            step2.append(copy(src, from_plane.at[i, e], send2.at[i, e], recv2.at[i, e], dev(xx, yy, z, core)))
    for i in range(2):
        total = acc_s[i, pl.ds(pl.multiple_of(place * PIECE, 8), PIECE), :]
        for n, e in enumerate(order):
            step2[15 * i + n].wait_recv()
            total = total + from_plane[i, e]
        from_line[i, z] = total
        for e in (4, 3, 5, 2, 6, 1, 7):
            ref = from_line.at[i, z]
            step3.append(copy(ref, ref, send3.at[i, e], recv3.at[i, e], dev(x, y, (z + e) % 8, core)))
    for i in range(2):
        for c in step3[7 * i : 7 * i + 7]:
            c.wait_recv()
        total = from_line[i, 0]
        for e in range(1, 8):
            total = total + from_line[i, e]
        at = rows(i, core, place * PIECE, PIECE)
        out_ref[at, :] = total
        ref = out_ref.at[at]
        for e in order:
            step4.append(copy(ref, ref, send4.at[i, e], recv4.at[i, e], dev(*plane(e), z, core)))
        step5.append(copy(ref, ref, send5.at[i, 0], recv5.at[i, 0], sibling))
    for i in range(2):
        for n, e in reversed(list(enumerate(order))):
            step4[15 * i + n].wait_recv()
            xx, yy = (x + 4 - e // 4) % 4, (y + 4 - e % 4) % 4
            ref = out_ref.at[rows(i, core, (xx * 4 + yy) * PIECE, PIECE)]
            step5.append(copy(ref, ref, send5.at[i, e], recv5.at[i, e], sibling))
    for c in step5:
        c.wait_recv()
    for c in step1 + step2 + step3 + step4 + step5:
        c.wait_send()


def dot(a, b, dims=(((1,), (0,)), ((), ()))):
    return lax.dot_general(a, b, dims, precision=lax.Precision.HIGHEST, preferred_element_type=F32)


def invert(m):
    lane = lax.broadcasted_iota(jnp.int32, (8, 128), 1)
    sub = lax.broadcasted_iota(jnp.int32, (8, 128), 0)
    def col(v, c):
        return jnp.broadcast_to(v[:, c:c + 1], (8, 128))
    def rowb(v, c):
        return jnp.broadcast_to(v[c:c + 1, :], (8, 128))
    for p in range(16):
        b = m[p]
        v = [col(b, 8 * p + c) for c in range(8)]
        for c in range(8):
            d = 1.0 / rowb(v[c], c)
            here = sub == c
            for e in range(c + 1, 8):
                r = rowb(v[e], c)
                v[e] = jnp.where(here, v[e] * d, v[e] - (v[c] * r) * d)
            at = lane == 8 * p + c
            r = jnp.where(at, 1.0, rowb(b, c)) * d
            b = jnp.where(here, r, jnp.where(at, 0.0, b) - v[c] * r)
        rows = [rowb(b, c) for c in range(8)]
        panel = (lane >= 8 * p) & (lane < 8 * p + 8)
        order = [i % 16 for i in range(p + 1, p + 16)]
        new = list(m)
        new[p] = b
        for i in order:
            terms = [col(m[i], 8 * p + c) * rows[c] for c in range(8)]
            while len(terms) > 1:
                terms = [x + y for x, y in zip(terms[::2], terms[1::2])]
            new[i] = jnp.where(panel, 0.0, m[i]) - terms[0]
        m = new
    return m

def solve(red_ref, a_s, w_s):
    lane = lax.broadcasted_iota(jnp.int32, (64, 128), 1)
    sub = lax.broadcasted_iota(jnp.int32, (64, 128), 0)
    where = {pair: n for n, pair in enumerate(HALVES)}

    def half(j, jj, side):
        n = where[j, jj]
        v = jnp.concatenate([red_ref[pl.ds(768 * i + 32 * (n // 2), 32), :] for i in range(2)], axis=0)
        return v if n % 2 == side else pltpu.roll(v, 64, 1)

    for j in range(8):
        for pair in range(j // 2, 5):
            if pair == 4:
                r = jnp.broadcast_to(red_ref[pl.ds(704 + j, 1), :], (64, 128))
                drive = jnp.sum(jnp.where(lane == sub, r, 0.0), axis=1, keepdims=True)
                u = jnp.where(lane < 64, half(j, 8, 0), jnp.where(lane == 64, drive, 0.0))
            elif 2 * pair < j:
                t = a_s[pl.ds(64 * j - 64, 64), pl.ds(128 * pair, 128)]
                t = jnp.concatenate([t, t], axis=0).T[64:]
                u = jnp.where(lane < 64, t, half(j, j, 1))
            else:
                u = jnp.where(lane < 64, half(j, 2 * pair, 0), half(j, 2 * pair + 1, 1))
            if pair == j // 2:
                u = jnp.where(lane == sub + 64 * (j % 2), u + 511.0, u)
            a_s[pl.ds(64 * j, 64), pl.ds(128 * pair, 128)] = u
    for k in range(4):
        at = 128 * k
        m = [a_s[pl.ds(at + 8 * i, 8), pl.ds(at, 128)] for i in range(16)]
        inv = jnp.concatenate(invert(m), axis=0)
        w = dot(inv, a_s[pl.ds(at, 128), pl.ds(at + 128, 512 - at)])
        w_s[pl.ds(at, 128), pl.ds(at + 128, 512 - at)] = w
        for i in range(k + 1, 4):
            ki = a_s[pl.ds(at, 128), pl.ds(128 * i, 128)]
            a_s[pl.ds(128 * i, 128), pl.ds(128 * i, 640 - 128 * i)] -= dot(
                ki, w[:, 128 * (i - k - 1):], (((0,), (0,)), ((), ())))
    for k in (2, 1, 0):
        at = 128 * k
        w_s[pl.ds(at, 128), pl.ds(512, 128)] -= dot(
            w_s[pl.ds(at, 128), pl.ds(at + 128, 384 - at)], w_s[pl.ds(at + 128, 384 - at), pl.ds(512, 128)])


def update_kernel(red_hbm, modes_ref, mem_hbm, inc_ref, ana_hbm, red_s, a_s, w_s, phi_s, u_s, big_s, mem_s, ana_s, red_sem, load_sem, save_sem):
    red_load = pltpu.make_async_copy(red_hbm, red_s, red_sem)
    red_load.start()
    load = pltpu.make_async_copy(mem_hbm, mem_s, load_sem)
    load.start()
    red_load.wait()
    solve(red_s, a_s, w_s)
    shift = lax.rem(128 - lax.axis_index("band") * 16, 128)
    phi = pltpu.roll(modes_ref[...], shift, 1)
    lane = lax.broadcasted_iota(jnp.int32, (8, 128), 1)
    for width in (16, 32, 64):
        phi = jnp.where(lane < width, phi, jnp.where(lane < 2 * width, pltpu.roll(phi, width, 1), 0.0))
    member = lax.broadcasted_iota(jnp.int32, (64, 1024), 0)
    owner = lax.broadcasted_iota(jnp.int32, (64, 1024), 1) // 16
    for j in range(8):
        wide = jnp.concatenate([jnp.broadcast_to(phi[j : j + 1, :], (64, 128))] * 8, axis=1)
        phi_s[pl.ds(64 * j, 64), :] = jnp.where(member == owner, wide, 0.0)
    u_s[...] = dot(w_s[:, 512:640], phi_s[...], (((0,), (0,)), ((), ())))
    level = lax.broadcasted_iota(jnp.int32, (16, 1024), 1) % 16
    own = level == lax.broadcasted_iota(jnp.int32, (16, 1024), 0)

    def spread(k, _):
        row = jnp.broadcast_to(u_s[pl.ds(k, 1), :], (16, 1024))
        big_s[pl.ds(pl.multiple_of(k * 16, 16), 16), :] = jnp.where(own, row, 0.0).astype(BF)
        return 0

    lax.fori_loop(0, 65, spread, 0, unroll=5)
    load.wait()
    saves = []
    for i in range(4):
        cols = pl.ds(512 * i, 512)
        m = mem_s[:, cols]
        r = jnp.dot(big_s[...], m, preferred_element_type=F32)
        ana_s[:, cols] = (m.astype(F32) - r[:1024]).astype(BF)
        inc_ref[:, cols] = r[1024:]
        save = pltpu.make_async_copy(ana_s.at[:, cols], ana_hbm.at[:, cols], save_sem.at[i])
        save.start()
        saves.append(save)
    for save in saves:
        save.wait()


def per_device(members, modes, *obs):
    flat = members.reshape(1024, 2048)
    in_hbm = pl.BlockSpec(memory_space=pl.ANY)
    red = pl.pallas_call(
        front_kernel,
        out_shape=jax.ShapeDtypeStruct((ROWS, 128), F32),
        in_specs=[in_hbm] * 7 + [pl.BlockSpec(memory_space=pltpu.SMEM)],
        out_specs=VM,
        scratch_shapes=[pltpu.VMEM((64, 128), jnp.int32)] * 3
        + [pltpu.VMEM((64, 128), F32)] * 3
        + [
            pltpu.VMEM((1024, 2048), BF),
            pltpu.VMEM((2, 896, 1024), BF),
            pltpu.VMEM((2, 256, 1024), BF),
            pltpu.VMEM((896, 256), F32),
            pltpu.VMEM((16, 64 * STRIDE + 8, 128), F32),
            pltpu.VMEM((2, 416, 2048), BF),
            pltpu.VMEM((9, 144, 128), F32),
            pltpu.VMEM((9, 64, 128), F32),
            pltpu.VMEM((3, 9, 9, 128), F32),
            pltpu.VMEM((2, 64, 2048), BF),
            pltpu.VMEM((2, 64, 2048), BF),
            pltpu.VMEM((ROWS, 128), F32),
            pltpu.VMEM((2, PART, 128), F32),
            pltpu.VMEM((2, PART, 128), F32),
            pltpu.VMEM((2, 16, PIECE, 128), F32),
            pltpu.VMEM((2, 8, PIECE, 128), F32),
            pltpu.SemaphoreType.DMA((6,)),
            pltpu.SemaphoreType.DMA,
        ]
        + [pltpu.SemaphoreType.DMA(n) for n in ((2,), (2,), (2,), (2,))]
        + [pltpu.SemaphoreType.DMA((2, n)) for n in (16, 16, 8, 8, 16, 16, 16, 16)],
        compiler_params=pltpu.CompilerParams(
            collective_id=0, has_side_effects=True, vmem_limit_bytes=60 * 2**20
        ),
        name="front",
    )(*[o.reshape(64, 128) for o in obs], flat, modes)
    inc, ana = pl.pallas_call(
        update_kernel,
        out_shape=(jax.ShapeDtypeStruct((16, 2048), F32), jax.ShapeDtypeStruct((1024, 2048), BF)),
        in_specs=[in_hbm, VM, in_hbm],
        out_specs=(VM, in_hbm),
        scratch_shapes=[
            pltpu.VMEM((ROWS, 128), F32),
            pltpu.VMEM((512, 640), F32),
            pltpu.VMEM((512, 640), F32),
            pltpu.VMEM((512, 1024), F32),
            pltpu.VMEM((128, 1024), F32),
            pltpu.VMEM((1040, 1024), BF),
            pltpu.VMEM((1024, 2048), BF),
            pltpu.VMEM((1024, 2048), BF),
            pltpu.SemaphoreType.DMA,
            pltpu.SemaphoreType.DMA,
            pltpu.SemaphoreType.DMA((4,)),
        ],
        compiler_params=pltpu.CompilerParams(vmem_limit_bytes=60 * 2**20),
        name="update",
    )(red, modes, flat)
    return inc, ana.reshape(64, 16, 2048)


def solution(mesh):
    placed = (
        P(None, "band", "tile"),
        P(),
        P(("tile", "band")),
        P(("tile", "band")),
        P(("tile", "band")),
        P(("tile", "band")),
        P(("tile", "band")),
        P(("tile", "band")),
    )
    return jax.shard_map(
        per_device,
        mesh=mesh,
        in_specs=placed,
        out_specs=(P("band", "tile"), P(None, "band", "tile")),
        check_vma=False,
    )
```

```python
import jax
import jax.numpy as jnp
from jax import lax
from jax.experimental import pallas as pl
from jax.experimental.pallas import tpu as pltpu
from jax.sharding import PartitionSpec as P

BF = jnp.bfloat16
F32 = jnp.float32
VM = pl.BlockSpec(memory_space=pltpu.VMEM)
NT = (((1,), (1,)), ((), ()))
STRIDE = 24
ROWS = 1536
PART = ROWS // 4
PIECE = PART // 16


def convert(mem_s, x32_s):
    def conv(m, _):
        v = mem_s[pl.ds(pl.multiple_of(m * 16, 16), 16), :].astype(F32)
        for k in range(16):
            x32_s[k, pl.ds(pl.multiple_of(m * STRIDE + 8, 8), 16), :] = v[:, 128 * k : 128 * k + 128]
        return 0
    lax.fori_loop(0, 64, conv, 0, unroll=2)


def scatter(obs_s, field_s, lhs_s, hot_s):
    cell_s, level_s, side_s, weight_s, scale_s, innov_s = obs_s
    rows16 = lax.broadcasted_iota(jnp.int32, (16, 128), 0).astype(F32)
    zero = jnp.zeros((16, 128), BF)
    one = jnp.ones((16, 128), BF)

    def split(v):
        hi = v.astype(BF).astype(F32)
        return hi, v - hi

    def fill(i, slot):
        sl = pl.ds(pl.multiple_of(i * 8, 8), 8)
        cell = cell_s[sl, :]
        lev = level_s[sl, :]
        side = side_s[sl, :]
        w = weight_s[sl, :]
        s = scale_s[sl, :]
        ch = cell >> 8
        keys = [
            (cell & 255).astype(F32),
            ((lev + 1) * 8 + ch).astype(F32),
            ((lev + 2 * side) * 8 + ch).astype(F32),
            ((lev + side + 1) * 8 + ch).astype(F32),
        ]
        a = s * (1.0 - w)
        b = s * w
        t = s * innov_s[sl, :]
        vals = [x for v in (a * a, b * b, a * b, a * t, b * t) for x in split(v)]
        for k in range(8):
            cols = slice(128 * k, 128 * k + 128)

            def wide(v):
                return jnp.broadcast_to(v[k : k + 1, :], (16, 128)).astype(BF)

            cl, kn, kf, kp = [wide(v) for v in keys]
            dn0, dn1, df0, df1, e0, e1, gn0, gn1, gf0, gf1 = [wide(v) for v in vals]
            for g in range(10):
                it = (rows16 + 16.0 * g).astype(BF)
                at = 16 * g
                if g < 9:
                    mn = it == kn
                    mf = it == kf
                    lhs_s[slot, pl.ds(at, 16), cols] = jnp.where(mn, dn0, jnp.where(mf, df0, zero))
                    lhs_s[slot, pl.ds(144 + at, 16), cols] = jnp.where(mn, dn1, jnp.where(mf, df1, zero))
                    lhs_s[slot, pl.ds(288 + at, 16), cols] = jnp.where(mn, gn0, jnp.where(mf, gf0, zero))
                    lhs_s[slot, pl.ds(432 + at, 16), cols] = jnp.where(mn, gn1, jnp.where(mf, gf1, zero))
                mp = it == kp
                lhs_s[slot, pl.ds(576 + at, 16), cols] = jnp.where(mp, e0, zero)
                lhs_s[slot, pl.ds(736 + at, 16), cols] = jnp.where(mp, e1, zero)
            for g in range(16):
                it = (rows16 + 16.0 * g).astype(BF)
                hot_s[slot, pl.ds(16 * g, 16), cols] = jnp.where(it == cl, one, zero)

    def add(slot):
        field_s[...] += lax.dot_general(lhs_s[slot], hot_s[slot], NT, preferred_element_type=F32)

    fill(0, 0)

    def steps(i, _):
        fill(2 * i + 1, 1)
        add(0)
        fill(2 * i + 2, 0)
        add(1)
        return 0

    lax.fori_loop(0, 3, steps, 0)
    fill(7, 1)
    add(0)
    add(1)


def products(ends, field_s, x32_s, stack_s, prod_s):
    first = lax.broadcasted_iota(jnp.int32, (16, 128), 0)
    lane = lax.broadcasted_iota(jnp.int32, (144, 128), 1)

    def field(base, step, r):
        at = pl.multiple_of(base + 8 * r, 8)
        return field_s[pl.ds(at, 8), :] + field_s[pl.ds(pl.multiple_of(at + step, 8), 8), :]

    def fill(q, slot):
        r = 2 * q
        below = jnp.maximum(r - 1, 0)
        ed = [field(576, 160, r + i) for i in range(2)]
        dd = [field(0, 144, r + i) for i in range(2)]
        gd = [field(288, 144, r + i) for i in range(2)]
        for k in range(16):
            cs = slice(128 * k, 128 * k + 128)

            def row(v):
                return v[k // 2 : k // 2 + 1, 128 * (k % 2) : 128 * (k % 2) + 128]

            xs = [x32_s[k, pl.ds(7 + l, 64, stride=STRIDE), :] for l in (below, r, r + 1)]
            for h in range(2):
                base = 144 * h
                stack_s[slot, pl.ds(288 + 64 * h, 64), cs] = xs[h + 1].astype(BF)
                stack_s[slot, pl.ds(base, 64), cs] = (xs[h + 1] * row(dd[h])).astype(BF)
                stack_s[slot, pl.ds(base + 64, 64), cs] = (xs[h] * row(ed[h])).astype(BF)
                g = jnp.broadcast_to(row(gd[h]), (16, 128))
                gh = g.astype(BF).astype(F32)
                both = jnp.where(first == 0, gh, jnp.where(first == 1, g - gh, 0.0))
                stack_s[slot, pl.ds(base + 128, 16), cs] = both.astype(BF)

    def multiply(q, slot):
        p = lax.dot_general(
            stack_s[slot, pl.ds(0, 288), :], stack_s[slot, pl.ds(288, 128), :], NT, preferred_element_type=F32
        )
        prod_s[q] = jnp.where(lane < 64, p[:144], p[144:])

    fill(1, 0)

    def steps(i, _):
        fill(2 * i + 2, 1)
        multiply(2 * i + 1, 0)
        fill(2 * i + 3, 0)
        multiply(2 * i + 2, 1)
        return 0

    lax.fori_loop(0, 3, steps, 0)
    multiply(7, 0)
    ends()
    fill(0, 0)
    fill(8, 1)
    multiply(0, 0)
    multiply(8, 1)


def coefs(modes_ref, start, coef_s):
    half = lax.broadcasted_iota(jnp.int32, (1, 128), 1) < 64
    for j in range(9):
        if j < 8:
            phi = []
            for r in range(-1, 19):
                l = start + r
                ok = (l >= 0) & (l < 128)
                phi.append(jnp.where(ok, modes_ref[j, jnp.clip(l, 0, 127)], 0.0))
        else:
            phi = [jnp.float32(1.0)] * 20
        for q in range(9):
            for s in range(3):
                r = 2 * q + (1, 0, 2)[s]
                coef_s[s, j, pl.ds(q, 1), :] = jnp.where(half, phi[r], phi[r + 1])


HALVES = [(j, jj) for j in range(8) for jj in range(j, 9)]


def levels_above(prod_s, above_s):
    left64 = lax.broadcasted_iota(jnp.int32, (64, 128), 1) < 64

    def transpose(q, _):
        above = jnp.minimum(q + 1, 8)
        t = jnp.concatenate([prod_s[q, pl.ds(64, 64), :], prod_s[above, pl.ds(64, 64), :]], axis=0).T
        right = jnp.where(q < 8, t[:64], 0.0)
        above_s[q] = jnp.where(left64, t[64:], right)
        return 0

    lax.fori_loop(0, 9, transpose, 0)


def expand(part, prod_s, above_s, coef_s, out_ref):
    base = part * 768
    lane8 = lax.broadcasted_iota(jnp.int32, (8, 128), 1) < 64

    def group(i, _):
        at = pl.multiple_of(part * 32 + i * 8, 8)
        s0 = [prod_s[q, pl.ds(at, 8), :] for q in range(9)]
        s1 = [prod_s[q, pl.ds(pl.multiple_of(64 + at, 8), 8), :] for q in range(9)]
        s2 = [above_s[q, pl.ds(at, 8), :] for q in range(9)]
        held, t = None, None
        for n, (j, jj) in enumerate(HALVES):
            if jj == j:
                t = [
                    s0[q] * coef_s[0, j, pl.ds(q, 1), :]
                    + s1[q] * coef_s[1, j, pl.ds(q, 1), :]
                    + s2[q] * coef_s[2, j, pl.ds(q, 1), :]
                    for q in range(9)
                ]
            acc = t[0] * coef_s[0, jj, pl.ds(0, 1), :]
            for q in range(1, 9):
                acc = acc + t[q] * coef_s[0, jj, pl.ds(q, 1), :]
            acc = acc + pltpu.roll(acc, 64, 1)
            if n % 2 == 0:
                held = acc
            else:
                out_ref[pl.ds(pl.multiple_of(base + n // 2 * 32 + i * 8, 8), 8), :] = jnp.where(lane8, held, acc)
        return 0

    lax.fori_loop(0, 4, group, 0)
    out_ref[pl.ds(base + 704, 64), :] = jnp.zeros((64, 128), F32)
    if part > 0:
        return
    for j in range(8):
        dr = jnp.zeros((1, 128), F32)
        for q in range(9):
            g = prod_s[q, pl.ds(128, 8), :]
            dr = dr + (g[0:1] + g[1:2]) * coef_s[0, j, pl.ds(q, 1), :]
        out_ref[pl.ds(704 + j, 1), :] = dr + pltpu.roll(dr, 64, 1)


def front_kernel(
    cell_h, level_h, side_h, weight_h, scale_h, innov_h, mem_h, modes_ref, out_ref,
    cell_s, level_s, side_s, weight_s, scale_s, innov_s, mem_s, lhs_s, hot_s, field_s, x32_s, stack_s, prod_s, above_s,
    coef_s, edge_s, halo_s, part_s, from_core, acc_s, from_plane, from_line,
    obs_sem, mem_sem, send0, recv0, send1, recv1, send2, recv2, send3, recv3, send4, recv4, send5, recv5,
):
    tile = lax.axis_index("tile")
    band = lax.axis_index("band")
    x, z, y, core = tile // 8, tile % 8, band // 2, band % 2

    def dev(xx, yy, zz, cc):
        return (xx * 8 + zz, yy * 2 + cc)

    def plane(e):
        return (x + e // 4) % 4, (y + e % 4) % 4

    order = sorted(range(1, 16), key=lambda e: -(min(e // 4, 4 - e // 4) + min(e % 4, 4 - e % 4)))
    sibling = dev(x, y, z, 1 - core)
    up = (tile, (band + 1) % 8)
    down = (tile, (band + 7) % 8)
    partners = [dev(x, y, (z + e) % 8, core) for e in (4, 3, 5)]
    for e in order:
        partners.append(dev(*plane(e), z, core))
    for e in (2, 6, 1, 7):
        partners.append(dev(x, y, (z + e) % 8, core))
    partners += [up, down]
    barrier = pltpu.get_barrier_semaphore()
    for d in partners:
        pl.semaphore_signal(barrier, inc=1, device_id=d, device_id_type=pl.DeviceIdType.MESH)

    obs_s = (cell_s, level_s, side_s, weight_s, scale_s, innov_s)
    loads = []
    for n, (h, s) in enumerate(zip((cell_h, level_h, side_h, weight_h, scale_h, innov_h), obs_s)):
        c = pltpu.make_async_copy(h, s, obs_sem.at[n])
        c.start()
        loads.append(c)
    mem_load = pltpu.make_async_copy(mem_h, mem_s, mem_sem)
    mem_load.start()
    coefs(modes_ref, band * 16 - 1, coef_s)
    field_s[...] = jnp.zeros_like(field_s)
    for c in loads:
        c.wait()
    scatter(obs_s, field_s, lhs_s, hot_s)
    mem_load.wait()
    convert(mem_s, x32_s)
    for k in range(16):
        cs = slice(128 * k, 128 * k + 128)
        edge_s[0, :, cs] = x32_s[k, pl.ds(8, 64, stride=STRIDE), :].astype(BF)
        edge_s[1, :, cs] = x32_s[k, pl.ds(23, 64, stride=STRIDE), :].astype(BF)
    pl.semaphore_wait(barrier, len(partners))

    def copy(src, dst, ss, rs, d):
        c = pltpu.make_async_remote_copy(
            src_ref=src, dst_ref=dst, send_sem=ss, recv_sem=rs, device_id=d, device_id_type=pl.DeviceIdType.MESH
        )
        c.start()
        return c

    halo = [
        copy(edge_s.at[0], halo_s.at[1], send0.at[0], recv0.at[0], down),
        copy(edge_s.at[1], halo_s.at[0], send0.at[1], recv0.at[1], up),
    ]
    def ends():
        for c in halo:
            c.wait()
        for k in range(16):
            cs = slice(128 * k, 128 * k + 128)
            x32_s[k, pl.ds(7, 64, stride=STRIDE), :] = jnp.where(band > 0, halo_s[0, :, cs].astype(F32), 0.0)
            x32_s[k, pl.ds(24, 64, stride=STRIDE), :] = jnp.where(band < 7, halo_s[1, :, cs].astype(F32), 0.0)

    products(ends, field_s, x32_s, stack_s, prod_s)

    place = x * 4 + y

    def rows(i, whose, at, n):
        return pl.ds(pl.multiple_of((2 * i + whose) * PART + at, 8), n)

    step1, step2, step3, step4, step5 = [], [], [], [], []
    levels_above(prod_s, above_s)
    for i in range(2):
        expand(i, prod_s, above_s, coef_s, part_s)
        ref = part_s.at[rows(i, 1 - core, 0, PART)]
        step1.append(copy(ref, from_core.at[i], send1.at[i], recv1.at[i], sibling))
    for i in range(2):
        step1[i].wait_recv()
        acc_s[i] = part_s[rows(i, core, 0, PART), :] + from_core[i]
        for e in order:
            xx, yy = plane(e)
            src = acc_s.at[i, pl.ds(pl.multiple_of((xx * 4 + yy) * PIECE, 8), PIECE)]
            step2.append(copy(src, from_plane.at[i, e], send2.at[i, e], recv2.at[i, e], dev(xx, yy, z, core)))
    for i in range(2):
        total = acc_s[i, pl.ds(pl.multiple_of(place * PIECE, 8), PIECE), :]
        for n, e in enumerate(order):
            step2[15 * i + n].wait_recv()
            total = total + from_plane[i, e]
        from_line[i, z] = total
        for e in (4, 3, 5, 2, 6, 1, 7):
            ref = from_line.at[i, z]
            step3.append(copy(ref, ref, send3.at[i, e], recv3.at[i, e], dev(x, y, (z + e) % 8, core)))
    for i in range(2):
        for c in step3[7 * i : 7 * i + 7]:
            c.wait_recv()
        total = from_line[i, 0]
        for e in range(1, 8):
            total = total + from_line[i, e]
        at = rows(i, core, place * PIECE, PIECE)
        out_ref[at, :] = total
        ref = out_ref.at[at]
        for e in order:
            step4.append(copy(ref, ref, send4.at[i, e], recv4.at[i, e], dev(*plane(e), z, core)))
        step5.append(copy(ref, ref, send5.at[i, 0], recv5.at[i, 0], sibling))
    for i in range(2):
        for n, e in reversed(list(enumerate(order))):
            step4[15 * i + n].wait_recv()
            xx, yy = (x + 4 - e // 4) % 4, (y + 4 - e % 4) % 4
            ref = out_ref.at[rows(i, core, (xx * 4 + yy) * PIECE, PIECE)]
            step5.append(copy(ref, ref, send5.at[i, e], recv5.at[i, e], sibling))
    for c in step5:
        c.wait_recv()
    for c in step1 + step2 + step3 + step4 + step5:
        c.wait_send()


def dot(a, b, dims=(((1,), (0,)), ((), ()))):
    return lax.dot_general(a, b, dims, precision=lax.Precision.HIGHEST, preferred_element_type=F32)


def invert(m):
    lane = lax.broadcasted_iota(jnp.int32, (8, 128), 1)
    sub = lax.broadcasted_iota(jnp.int32, (8, 128), 0)
    def col(v, c):
        return jnp.broadcast_to(v[:, c:c + 1], (8, 128))
    def rowb(v, c):
        return jnp.broadcast_to(v[c:c + 1, :], (8, 128))
    for p in range(16):
        b = m[p]
        v = [col(b, 8 * p + c) for c in range(8)]
        for c in range(8):
            d = 1.0 / rowb(v[c], c)
            here = sub == c
            for e in range(c + 1, 8):
                r = rowb(v[e], c)
                v[e] = jnp.where(here, v[e] * d, v[e] - (v[c] * r) * d)
            at = lane == 8 * p + c
            r = jnp.where(at, 1.0, rowb(b, c)) * d
            b = jnp.where(here, r, jnp.where(at, 0.0, b) - v[c] * r)
        rows = [rowb(b, c) for c in range(8)]
        panel = (lane >= 8 * p) & (lane < 8 * p + 8)
        order = [i % 16 for i in range(p + 1, p + 16)]
        new = list(m)
        new[p] = b
        for i in order:
            terms = [col(m[i], 8 * p + c) * rows[c] for c in range(8)]
            while len(terms) > 1:
                terms = [x + y for x, y in zip(terms[::2], terms[1::2])]
            new[i] = jnp.where(panel, 0.0, m[i]) - terms[0]
        m = new
    return m

def solve(red_ref, a_s, w_s):
    lane = lax.broadcasted_iota(jnp.int32, (64, 128), 1)
    sub = lax.broadcasted_iota(jnp.int32, (64, 128), 0)
    where = {pair: n for n, pair in enumerate(HALVES)}

    def half(j, jj, side):
        n = where[j, jj]
        v = jnp.concatenate([red_ref[pl.ds(768 * i + 32 * (n // 2), 32), :] for i in range(2)], axis=0)
        return v if n % 2 == side else pltpu.roll(v, 64, 1)

    for j in range(8):
        for pair in range(j // 2, 5):
            if pair == 4:
                r = jnp.broadcast_to(red_ref[pl.ds(704 + j, 1), :], (64, 128))
                drive = jnp.sum(jnp.where(lane == sub, r, 0.0), axis=1, keepdims=True)
                u = jnp.where(lane < 64, half(j, 8, 0), jnp.where(lane == 64, drive, 0.0))
            elif 2 * pair < j:
                t = a_s[pl.ds(64 * j - 64, 64), pl.ds(128 * pair, 128)]
                t = jnp.concatenate([t, t], axis=0).T[64:]
                u = jnp.where(lane < 64, t, half(j, j, 1))
            else:
                u = jnp.where(lane < 64, half(j, 2 * pair, 0), half(j, 2 * pair + 1, 1))
            if pair == j // 2:
                u = jnp.where(lane == sub + 64 * (j % 2), u + 511.0, u)
            a_s[pl.ds(64 * j, 64), pl.ds(128 * pair, 128)] = u
    for k in range(4):
        at = 128 * k
        m = [a_s[pl.ds(at + 8 * i, 8), pl.ds(at, 128)] for i in range(16)]
        inv = jnp.concatenate(invert(m), axis=0)
        w = dot(inv, a_s[pl.ds(at, 128), pl.ds(at + 128, 512 - at)])
        w_s[pl.ds(at, 128), pl.ds(at + 128, 512 - at)] = w
        for i in range(k + 1, 4):
            ki = a_s[pl.ds(at, 128), pl.ds(128 * i, 128)]
            a_s[pl.ds(128 * i, 128), pl.ds(128 * i, 640 - 128 * i)] -= dot(
                ki, w[:, 128 * (i - k - 1):], (((0,), (0,)), ((), ())))
    for k in (2, 1, 0):
        at = 128 * k
        w_s[pl.ds(at, 128), pl.ds(512, 128)] -= dot(
            w_s[pl.ds(at, 128), pl.ds(at + 128, 384 - at)], w_s[pl.ds(at + 128, 384 - at), pl.ds(512, 128)])


def update_kernel(red_hbm, modes_ref, mem_hbm, inc_ref, ana_hbm, red_s, a_s, w_s, phi_s, u_s, big_s, mem_s, ana_s, red_sem, load_sem, save_sem):
    red_load = pltpu.make_async_copy(red_hbm, red_s, red_sem)
    red_load.start()
    load = pltpu.make_async_copy(mem_hbm, mem_s, load_sem)
    load.start()
    red_load.wait()
    solve(red_s, a_s, w_s)
    shift = lax.rem(128 - lax.axis_index("band") * 16, 128)
    phi = pltpu.roll(modes_ref[...], shift, 1)
    lane = lax.broadcasted_iota(jnp.int32, (8, 128), 1)
    for width in (16, 32, 64):
        phi = jnp.where(lane < width, phi, jnp.where(lane < 2 * width, pltpu.roll(phi, width, 1), 0.0))
    member = lax.broadcasted_iota(jnp.int32, (64, 1024), 0)
    owner = lax.broadcasted_iota(jnp.int32, (64, 1024), 1) // 16
    for j in range(8):
        wide = jnp.concatenate([jnp.broadcast_to(phi[j : j + 1, :], (64, 128))] * 8, axis=1)
        phi_s[pl.ds(64 * j, 64), :] = jnp.where(member == owner, wide, 0.0)
    u_s[...] = dot(w_s[:, 512:640], phi_s[...], (((0,), (0,)), ((), ())))
    level = lax.broadcasted_iota(jnp.int32, (16, 1024), 1) % 16
    own = level == lax.broadcasted_iota(jnp.int32, (16, 1024), 0)

    def spread(k, _):
        row = jnp.broadcast_to(u_s[pl.ds(k, 1), :], (16, 1024))
        big_s[pl.ds(pl.multiple_of(k * 16, 16), 16), :] = jnp.where(own, row, 0.0).astype(BF)
        return 0

    lax.fori_loop(0, 65, spread, 0, unroll=5)
    load.wait()
    saves = []
    for i in range(4):
        cols = pl.ds(512 * i, 512)
        m = mem_s[:, cols]
        r = jnp.dot(big_s[...], m, preferred_element_type=F32)
        ana_s[:, cols] = (m.astype(F32) - r[:1024]).astype(BF)
        inc_ref[:, cols] = r[1024:]
        save = pltpu.make_async_copy(ana_s.at[:, cols], ana_hbm.at[:, cols], save_sem.at[i])
        save.start()
        saves.append(save)
    for save in saves:
        save.wait()


def per_device(members, modes, *obs):
    flat = members.reshape(1024, 2048)
    in_hbm = pl.BlockSpec(memory_space=pl.ANY)
    red = pl.pallas_call(
        front_kernel,
        out_shape=jax.ShapeDtypeStruct((ROWS, 128), F32),
        in_specs=[in_hbm] * 7 + [pl.BlockSpec(memory_space=pltpu.SMEM)],
        out_specs=VM,
        scratch_shapes=[pltpu.VMEM((64, 128), jnp.int32)] * 3
        + [pltpu.VMEM((64, 128), F32)] * 3
        + [
            pltpu.VMEM((1024, 2048), BF),
            pltpu.VMEM((2, 896, 1024), BF),
            pltpu.VMEM((2, 256, 1024), BF),
            pltpu.VMEM((896, 256), F32),
            pltpu.VMEM((16, 64 * STRIDE + 8, 128), F32),
            pltpu.VMEM((2, 416, 2048), BF),
            pltpu.VMEM((9, 144, 128), F32),
            pltpu.VMEM((9, 64, 128), F32),
            pltpu.VMEM((3, 9, 9, 128), F32),
            pltpu.VMEM((2, 64, 2048), BF),
            pltpu.VMEM((2, 64, 2048), BF),
            pltpu.VMEM((ROWS, 128), F32),
            pltpu.VMEM((2, PART, 128), F32),
            pltpu.VMEM((2, PART, 128), F32),
            pltpu.VMEM((2, 16, PIECE, 128), F32),
            pltpu.VMEM((2, 8, PIECE, 128), F32),
            pltpu.SemaphoreType.DMA((6,)),
            pltpu.SemaphoreType.DMA,
        ]
        + [pltpu.SemaphoreType.DMA(n) for n in ((2,), (2,), (2,), (2,))]
        + [pltpu.SemaphoreType.DMA((2, n)) for n in (16, 16, 8, 8, 16, 16, 16, 16)],
        compiler_params=pltpu.CompilerParams(
            collective_id=0, has_side_effects=True, vmem_limit_bytes=60 * 2**20
        ),
        name="front",
    )(*[o.reshape(64, 128) for o in obs], flat, modes)
    inc, ana = pl.pallas_call(
        update_kernel,
        out_shape=(jax.ShapeDtypeStruct((16, 2048), F32), jax.ShapeDtypeStruct((1024, 2048), BF)),
        in_specs=[in_hbm, VM, in_hbm],
        out_specs=(VM, in_hbm),
        scratch_shapes=[
            pltpu.VMEM((ROWS, 128), F32),
            pltpu.VMEM((512, 640), F32),
            pltpu.VMEM((512, 640), F32),
            pltpu.VMEM((512, 1024), F32),
            pltpu.VMEM((128, 1024), F32),
            pltpu.VMEM((1040, 1024), BF),
            pltpu.VMEM((1024, 2048), BF),
            pltpu.VMEM((1024, 2048), BF),
            pltpu.SemaphoreType.DMA,
            pltpu.SemaphoreType.DMA,
            pltpu.SemaphoreType.DMA((4,)),
        ],
        compiler_params=pltpu.CompilerParams(vmem_limit_bytes=60 * 2**20),
        name="update",
    )(red, modes, flat)
    return inc, ana.reshape(64, 16, 2048)


def solution(mesh):
    placed = (
        P(None, "band", "tile"),
        P(),
        P(("tile", "band")),
        P(("tile", "band")),
        P(("tile", "band")),
        P(("tile", "band")),
        P(("tile", "band")),
        P(("tile", "band")),
    )
    return jax.shard_map(
        per_device,
        mesh=mesh,
        in_specs=placed,
        out_specs=(P("band", "tile"), P(None, "band", "tile")),
        check_vma=False,
    )
```
